512 devices in a mesh: section: 8 (over y, core), peer: 64 (over x, z).
Axes of the slice: x: 4, y: 4, z: 16, core: 2. Of those that a mesh axis runs over, the one named last changes fastest.
Arguments:
- pending_activations: bfloat16 [8, 128, 2560], P('section', 'peer'), may hold values from -6 to 6
- new_first_inputs: bfloat16 [1, 128, 2560], P(None, 'peer'), may hold values from -6 to 6
- stored_section_inputs: bfloat16 [2, 8, 128, 2560], P(None, 'section', 'peer'), may hold values from -6 to 6
- pending_gradients: bfloat16 [8, 128, 2560], P('section', 'peer'), may hold values from -1.5 to 1.5
- loss_gradients: bfloat16 [1, 128, 2560], P(None, 'peer'), may hold values from -1.5 to 1.5
- forward_wiring: int32 [2, 8, 128], replicated, may hold values from 0 to 127, each once within a row
- backward_wiring: int32 [2, 8, 128], replicated, may hold values from 0 to 127, each once within a row
- norm_gain_vector: float32 [8, 2560], P('section'), may hold values from 0.25 to 1.75
- up_projection_weight: bfloat16 [8, 10240, 2560], P('section', 'peer'), may hold values from -0.125 to 0.125
- down_projection_weight: bfloat16 [8, 10240, 2560], P('section', 'peer'), may hold values from -0.0625 to 0.0625
Outputs:
- section_outputs: bfloat16 [2, 8, 128, 2560], P(None, 'section', 'peer')
- input_grads: bfloat16 [2, 8, 128, 2560], P(None, 'section', 'peer')
- up_grad: bfloat16 [8, 10240, 2560], P('section', 'peer')
- down_grad: bfloat16 [8, 10240, 2560], P('section', 'peer')
- gain_grad: float32 [8, 2560], P('section')
The draws below stay inside these ranges and needn't reach their ends.
Inputs may be any that keep to these rules, and one draw needn't show every extreme that they name: Each row of forward_wiring[k, s] names every received row once. Each row of backward_wiring[k, s] names every arrival position once.
All inputs are finite; a program needn't handle non-finite values.
Results may differ from the reference program's by a relative error of at most 0.007.
Values may be sent and summed in bfloat16 or wider, within the bound.
A program may use at most 64 MiB of HBM per device.

```python
import jax
import jax.numpy as jnp
from jax import lax

FEATURE_WIDTH = 2560
F = 10240
MICRO_TOKENS = 64
REPLICA_COUNT = 2
TICKS = 2
N_SECTION = 8


def steps_of(rng, extent, split, least, largest):
    loudness = 1.0
    for position, blocks in split:
        draws = jax.random.uniform(jax.random.fold_in(jax.random.fold_in(rng, 6), position), (blocks,), jnp.float32, least / len(split), largest / len(split))
        loudness = loudness * jnp.repeat(jnp.exp(draws), extent[position] // blocks).reshape((-1,) + (1,) * (len(extent) - 1 - position))
    return loudness


def normal_values(own_key, dims, scale, reach, cuts=(), held_as=jnp.bfloat16):
    result = scale * jax.random.normal(own_key, dims, jnp.float32)
    if cuts:
        result = result * steps_of(own_key, dims, cuts, -0.22, 0.18)
    return jnp.clip(result, -reach, reach).astype(held_as)


def setup_inputs(seed: int = 0) -> dict:
    key_list = jax.random.split(jax.random.key(seed), 11)
    pending_activations = normal_values(key_list[0], (N_SECTION, REPLICA_COUNT * MICRO_TOKENS, FEATURE_WIDTH), 1.0, 6.0, ((0, 8), (1, 64)))
    new_first_inputs = normal_values(key_list[1], (TICKS - 1, REPLICA_COUNT * MICRO_TOKENS, FEATURE_WIDTH), 1.0, 6.0, ((1, 64),))
    stored_section_inputs = normal_values(key_list[2], (TICKS, N_SECTION, REPLICA_COUNT * MICRO_TOKENS, FEATURE_WIDTH), 1.0, 6.0, ((1, 8), (2, 64)))
    pending_gradients = normal_values(key_list[3], (N_SECTION, REPLICA_COUNT * MICRO_TOKENS, FEATURE_WIDTH), 0.25, 1.5, ((0, 8), (1, 64)))
    loss_gradients = normal_values(key_list[4], (TICKS - 1, REPLICA_COUNT * MICRO_TOKENS, FEATURE_WIDTH), 0.25, 1.5, ((1, 64),))
    forward_wiring = jax.vmap(lambda own: jax.random.permutation(own, REPLICA_COUNT * MICRO_TOKENS))(jax.random.split(key_list[5], TICKS * N_SECTION)).reshape((TICKS, N_SECTION, REPLICA_COUNT * MICRO_TOKENS)).astype(jnp.int32)
    backward_wiring = jax.vmap(lambda own: jax.random.permutation(own, REPLICA_COUNT * MICRO_TOKENS))(jax.random.split(key_list[6], TICKS * N_SECTION)).reshape((TICKS, N_SECTION, REPLICA_COUNT * MICRO_TOKENS)).astype(jnp.int32)
    norm_gain_vector = jnp.clip(1.0 + 0.15 * jax.random.normal(key_list[7], (N_SECTION, FEATURE_WIDTH), jnp.float32), 0.25, 1.75)
    up_projection_weight = normal_values(key_list[8], (N_SECTION, F, FEATURE_WIDTH), FEATURE_WIDTH ** -0.5, 0.125, ((0, 8), (1, 64)))
    down_projection_weight = normal_values(key_list[9], (N_SECTION, F, FEATURE_WIDTH), F ** -0.5, 0.0625, ((0, 8), (1, 64)))
    return dict(pending_activations=pending_activations, new_first_inputs=new_first_inputs, stored_section_inputs=stored_section_inputs, pending_gradients=pending_gradients, loss_gradients=loss_gradients, forward_wiring=forward_wiring, backward_wiring=backward_wiring, norm_gain_vector=norm_gain_vector, up_projection_weight=up_projection_weight, down_projection_weight=down_projection_weight)


epsilon = 1e-05

def norm_parts(x, gain_row):
    as_float = x.astype(jnp.float32)
    inv_rms = lax.rsqrt(lax.optimization_barrier(jnp.mean(as_float * as_float, axis=-1, keepdims=True)) + epsilon)
    normed = (as_float * inv_rms * gain_row).astype(jnp.bfloat16)
    return (as_float, inv_rms, normed)

def up_project(normed, up_mat):
    return lax.dot_general(normed, up_mat, (((1,), (1,)), ((), ())), preferred_element_type=jnp.float32)

def inverse_order(route):
    count = route.shape[0]
    return jnp.zeros((count,), jnp.int32).at[route].set(jnp.arange(count, dtype=jnp.int32))

def section_forward(used, gain_row, up_mat, down_mat):
    as_float, inv_rms, normed = norm_parts(used, gain_row)
    hidden = jax.nn.silu(up_project(normed, up_mat)).astype(jnp.bfloat16)
    branch = jnp.dot(hidden, down_mat, preferred_element_type=jnp.float32)
    return (as_float + branch).astype(jnp.bfloat16)

def section_backward(saved, grad_out, gain_row, up_mat, down_mat):
    as_float, inv_rms, normed = norm_parts(saved, gain_row)
    pre_act = up_project(normed, up_mat)
    hidden = jax.nn.silu(pre_act).astype(jnp.bfloat16)
    d_hidden = lax.dot_general(grad_out, down_mat, (((1,), (1,)), ((), ())), preferred_element_type=jnp.float32)
    sigma = jax.nn.sigmoid(pre_act)
    d_pre = (d_hidden * sigma * (1.0 + pre_act * (1.0 - sigma))).astype(jnp.bfloat16)
    down_part = lax.dot_general(hidden, grad_out, (((0,), (0,)), ((), ())), preferred_element_type=jnp.float32)
    up_part = lax.dot_general(d_pre, normed, (((0,), (0,)), ((), ())), preferred_element_type=jnp.float32)
    d_normed = jnp.dot(d_pre, up_mat, preferred_element_type=jnp.float32)
    gain_part = lax.optimization_barrier(jnp.sum(d_normed * as_float * inv_rms, axis=0))
    scaled = d_normed * gain_row
    cube = inv_rms * inv_rms * inv_rms
    d_input = inv_rms * scaled - as_float * cube * lax.optimization_barrier(jnp.mean(scaled * as_float, axis=-1, keepdims=True))
    d_used = grad_out.astype(jnp.float32) + d_input
    return (d_used, up_part, down_part, gain_part)

def reference(pending_activations, new_first_inputs, stored_section_inputs, pending_gradients, loss_gradients, forward_wiring, backward_wiring, norm_gain_vector, up_projection_weight, down_projection_weight):
    section_count = N_SECTION
    received_rows = pending_activations
    incoming_gradients = pending_gradients
    acc_up = jnp.zeros(up_projection_weight.shape, jnp.float32)
    acc_down = jnp.zeros(down_projection_weight.shape, jnp.float32)
    acc_gain = jnp.zeros(norm_gain_vector.shape, jnp.float32)
    all_outputs = []
    all_grads = []
    for moment in range(TICKS):
        outputs = []
        grads = []
        for section_no in range(section_count):
            used = jnp.take(received_rows[section_no], forward_wiring[moment, section_no], axis=0)
            outputs.append(section_forward(used, norm_gain_vector[section_no], up_projection_weight[section_no], down_projection_weight[section_no]))
            d_used, up_part, down_part, gain_part = section_backward(stored_section_inputs[moment, section_no], incoming_gradients[section_no], norm_gain_vector[section_no], up_projection_weight[section_no], down_projection_weight[section_no])
            back_order = inverse_order(backward_wiring[moment, section_no])
            grads.append(jnp.take(d_used, back_order, axis=0).astype(jnp.bfloat16))
            acc_up = acc_up.at[section_no].add(up_part)
            acc_down = acc_down.at[section_no].add(down_part)
            acc_gain = acc_gain.at[section_no].add(gain_part)
        out_stack = jnp.stack(outputs)
        grad_stack = jnp.stack(grads)
        all_outputs.append(out_stack)
        all_grads.append(grad_stack)
        if moment + 1 < TICKS:
            received_rows = jnp.concatenate([new_first_inputs[moment][None], out_stack[:-1]], axis=0)
            incoming_gradients = jnp.concatenate([grad_stack[1:], loss_gradients[moment][None]], axis=0)
    share = 1.0 / REPLICA_COUNT
    return (jnp.stack(all_outputs), jnp.stack(all_grads), (acc_up * share).astype(jnp.bfloat16), (acc_down * share).astype(jnp.bfloat16), acc_gain)
```

```python
import jax
import jax.numpy as jnp
from jax import lax
from jax.experimental import pallas as pl
from jax.experimental.pallas import tpu as pltpu
from jax.sharding import PartitionSpec as P

MESH = pl.DeviceIdType.MESH
EPS = 1e-05
NX, NZ = 4, 16
ROWS = 128
BLOCKS = 20
WIDTH = BLOCKS * 128
LINES = 2 * BLOCKS
UNITS = 160
X0, DY0, ACT0, X1, ACT1, DY1 = range(6)
B0, F0, B1, F1 = range(4)
f32, bf16 = jnp.float32, jnp.bfloat16


def dot(a, b):
    return jnp.dot(a, b, preferred_element_type=f32)


def dot_t(a, b):
    return lax.dot_general(a, b, (((1,), (1,)), ((), ())), preferred_element_type=f32)


def cols(c, n=1):
    return pl.ds(c * 128, n * 128)


def kernel(
    act_ref, first_ref, stored_ref, pend_ref, loss_ref, fw_ref, bw_ref, gain_ref, up_hbm, down_hbm,
    out_ref, grad_ref, upg_hbm, downg_hbm, gaing_ref,
    up, down, gat, nat, xs, dys, normed, dyb, hid, dpre, part, part_in, fsum, wire, wire_in,
    pas, gpart, gx, gz, hot, upg, downg,
    w_sem, zs, zr, xsnd, xrcv, ps, pr, gs, gr, og_sem,
):
    sec = lax.axis_index("section")
    peer = lax.axis_index("peer")
    mx, mz = peer // NZ, lax.rem(peer, NZ)

    def at_z(d):
        return (sec, mx * NZ + lax.rem(mz + d, NZ))

    def at_x(d):
        return (sec, lax.rem(mx + d, NX) * NZ + mz)

    nxt = (lax.rem(sec + 1, 8), peer)
    prv = (lax.rem(sec + 7, 8), peer)

    load_up = pltpu.make_async_copy(up_hbm.at[0], up, w_sem.at[0])
    load_down = pltpu.make_async_copy(down_hbm.at[0], down, w_sem.at[1])
    load_up.start()
    load_down.start()

    barrier = pltpu.get_barrier_semaphore()

    def greet_z(d, _):
        pl.semaphore_signal(barrier, inc=1, device_id=at_z(d), device_id_type=MESH)
        return 0

    lax.fori_loop(1, NZ, greet_z, 0)
    for d in range(1, NX):
        pl.semaphore_signal(barrier, inc=1, device_id=at_x(d), device_id_type=MESH)
    for other in (nxt, prv):
        pl.semaphore_signal(barrier, inc=1, device_id=other, device_id_type=MESH)

    def lines_of(pair):
        flat = pair.astype(f32)
        return jnp.concatenate([flat[:, c * 128 : (c + 1) * 128] for c in range(BLOCKS)], axis=0).astype(bf16)

    gat[X0, 0, 0] = lines_of(stored_ref[0, 0])
    gat[DY0, 0, 0] = lines_of(pend_ref[0])
    gat[ACT0, 0, 0] = lines_of(act_ref[0])
    gat[X1, 0, 0] = lines_of(stored_ref[1, 0])
    pl.semaphore_wait(barrier, NZ - 1 + NX - 1 + 2)

    def z_gather(a):
        def send(n, _):
            step = (n + 1) // 2
            d = jnp.where(lax.rem(n, 2) == 1, NZ // 2 - step, NZ // 2 + step)
            pltpu.make_async_remote_copy(
                src_ref=gat.at[a, 0, 0], dst_ref=gat.at[a, 0, NZ - d], send_sem=zs.at[a], recv_sem=zr.at[a],
                device_id=at_z(d), device_id_type=MESH,
            ).start()
            return 0

        lax.fori_loop(0, NZ - 1, send, 0)

    def wait_bytes(ref, sem):
        pltpu.make_async_copy(ref, ref, sem).wait()

    def x_gather(a):
        wait_bytes(gat.at[a, 0, pl.ds(1, NZ - 1)], zr.at[a])
        for d in range(1, NX):
            pltpu.make_async_remote_copy(
                src_ref=gat.at[a, 0], dst_ref=gat.at[a, NX - d], send_sem=xsnd.at[a], recv_sem=xrcv.at[a],
                device_id=at_x(d), device_id_type=MESH,
            ).start()

    def natural(a, lo, hi):
        def one(q, _):
            nat[pl.ds(q, LINES, stride=64), :] = gat[a, q // NZ, lax.rem(q, NZ)].astype(f32)
            return 0

        lax.fori_loop(lo, hi, one, 0)

    def finish_gather(a):
        natural(a, 0, NZ)
        wait_bytes(gat.at[a, pl.ds(1, NX - 1)], xrcv.at[a])
        natural(a, NZ, NZ * NX)

    def row_of(index):
        i = index // 64
        xr = lax.rem(index, 64) // NZ
        zr_ = lax.rem(index, NZ)
        return 2 * (lax.rem(mx + xr, NX) * NZ + lax.rem(mz + zr_, NZ)) + i

    def one_hot(route):
        down_rows = row_of(lax.broadcasted_iota(jnp.int32, (ROWS, ROWS), 0))
        lane = lax.broadcasted_iota(jnp.int32, (ROWS, ROWS), 1)
        picked = jnp.sum(jnp.where(down_rows == lane, route.astype(f32), 0.0), axis=1, keepdims=True)
        return jnp.where(picked == row_of(lane).astype(f32), 1.0, 0.0)

    def permuted(index, dst):
        turn = hot[index]
        for c in range(0, BLOCKS, 2):
            both = jnp.concatenate([nat[pl.ds(c * 128, 128), :], nat[pl.ds(c * 128 + 128, 128), :]], axis=1)
            got = dot(turn, both.astype(bf16))
            dst[pl.ds(c * 128, 128), :] = got[:, :128]
            dst[pl.ds(c * 128 + 128, 128), :] = got[:, 128:]

    def norm(into):
        total = jnp.zeros((ROWS, 128), f32)
        for c in range(BLOCKS):
            block = xs[pl.ds(c * 128, 128), :]
            total = total + block * block
        inv = lax.rsqrt(jnp.sum(total, axis=1, keepdims=True) * (1.0 / WIDTH) + EPS)
        for c in range(BLOCKS):
            block = xs[pl.ds(c * 128, 128), :]
            into[:, c * 128 : (c + 1) * 128] = (block * inv * gain_ref[:, c * 128 : (c + 1) * 128]).astype(bf16)
        return inv

    def put_part(r, c, block):
        low = block.astype(bf16)
        for xr in range(NX):
            for i in range(2):
                part[r, xr, c, pl.ds(i * 16, 16), :] = low[i * 64 + xr * 16 : i * 64 + xr * 16 + 16, :]

    def x_sum(r):
        for d in range(1, NX):
            pltpu.make_async_remote_copy(
                src_ref=part.at[r, d], dst_ref=part_in.at[r, NX - 1 - d], send_sem=xsnd.at[6 + r], recv_sem=xrcv.at[6 + r],
                device_id=at_x(d), device_id_type=MESH,
            ).start()

    def z_sum(r):
        wait_bytes(part_in.at[r], xrcv.at[6 + r])

        def add(c, _):
            total = part[r, 0, c].astype(f32)
            for k in range(NX - 1):
                total = total + part_in[r, k, c].astype(f32)
            fsum[r, pl.ds(pl.multiple_of(c * 32, 32), 32), :] = total
            return 0

        lax.fori_loop(0, BLOCKS, add, 0)

        def send(n, _):
            step = (n + 1) // 2
            d = jnp.where(lax.rem(n, 2) == 1, NZ // 2 - step, NZ // 2 + step)
            wire[r, d] = fsum[r, pl.ds(d, LINES, stride=16), :].astype(bf16)
            pltpu.make_async_remote_copy(
                src_ref=wire.at[r, d], dst_ref=wire_in.at[r, NZ - d], send_sem=zs.at[6 + r], recv_sem=zr.at[6 + r],
                device_id=at_z(d), device_id_type=MESH,
            ).start()
            return 0

        lax.fori_loop(0, NZ - 1, send, 0)

    def finish_sum(r):
        wait_bytes(wire_in.at[r, pl.ds(1, NZ - 1)], zr.at[6 + r])
        total = fsum[r, pl.ds(0, LINES, stride=16), :]
        for k in range(1, NZ):
            total = total + wire_in[r, k].astype(f32)
        return total

    def own_lines(ref):
        return ref[pl.ds(0, LINES, stride=64), :]

    def forward(r, tick):
        permuted(tick, xs)
        norm(normed.at[2])
        pre = dot_t(normed[2], up[...])
        hidden = (pre / (1.0 + jnp.exp(-pre))).astype(bf16)
        for c in range(0, BLOCKS, 2):
            branch = dot(hidden, down[:, c * 128 : (c + 2) * 128])
            put_part(r, c, branch[:, :128])
            put_part(r, c + 1, branch[:, 128:])
        x_sum(r)
        return own_lines(xs)

    def backward_inputs(tick, a_x):
        permuted(2 + tick, xs)
        inv = norm(normed.at[tick])
        pre = dot_t(normed[tick], up[...])
        return inv, pre

    def backward(r, tick, inv, pre):
        permuted(2 + tick, dys)
        for c in range(BLOCKS):
            dyb[tick, :, c * 128 : (c + 1) * 128] = dys[pl.ds(c * 128, 128), :].astype(bf16)
        d_hidden = dot_t(dyb[tick], down[...])
        sig = 1.0 / (1.0 + jnp.exp(-pre))
        hid[:, tick * ROWS : (tick + 1) * ROWS] = (pre * sig).T.astype(bf16)
        d_pre = d_hidden * sig * (1.0 + pre * (1.0 - sig))
        dpre[:, tick * ROWS : (tick + 1) * ROWS] = d_pre.T.astype(bf16)
        d_pre = d_pre.astype(bf16)
        for c in range(0, BLOCKS, 2):
            d_norm = dot(d_pre, up[:, c * 128 : (c + 2) * 128])
            for k in range(2):
                block = d_norm[:, k * 128 : (k + 1) * 128]
                put_part(r, c + k, block)
                line = jnp.sum(block * (xs[pl.ds((c + k) * 128, 128), :] * inv), axis=0, keepdims=True)
                if tick == 0:
                    gpart[c + k : c + k + 1, :] = line
                else:
                    gpart[c + k : c + k + 1, :] += line
        x_sum(r)
        return own_lines(xs), own_lines(dys)

    even = lax.rem(lax.broadcasted_iota(jnp.int32, (LINES, 128), 0), 2) == 0

    def row_means(v):
        first = jnp.sum(jnp.where(even, v, 0.0), keepdims=True)
        second = jnp.sum(jnp.where(even, 0.0, v), keepdims=True)
        return jnp.where(even, first, second) * (1.0 / WIDTH)

    gain_lines = jnp.concatenate(
        [jnp.broadcast_to(gain_ref[:, c * 128 : (c + 1) * 128], (2, 128)) for c in range(BLOCKS)], axis=0
    )

    def input_grad(d_norm, x, dy):
        inv = lax.rsqrt(row_means(x * x) + EPS)
        scaled = d_norm * gain_lines
        return dy + inv * scaled - x * (inv * inv * inv) * row_means(scaled * x)

    def put_pair(ref, tick, value):
        for c in range(BLOCKS):
            ref[tick, 0, :, c * 128 : (c + 1) * 128] = value[2 * c : 2 * c + 2, :].astype(bf16)

    def hand_on(k, value, other, a):
        pas[k] = value
        pltpu.make_async_remote_copy(
            src_ref=pas.at[k], dst_ref=gat.at[a, 0, 0], send_sem=ps.at[k], recv_sem=pr.at[k],
            device_id=other, device_id_type=MESH,
        ).start()

    z_gather(X0)
    z_gather(DY0)
    z_gather(ACT0)
    for tick in range(2):
        hot[tick] = one_hot(fw_ref[tick, pl.ds(sec, 1), :]).astype(bf16)
        hot[2 + tick] = one_hot(bw_ref[tick, pl.ds(sec, 1), :]).T.astype(bf16)
    x_gather(X0)
    x_gather(DY0)
    x_gather(ACT0)
    z_gather(X1)
    load_up.wait()
    load_down.wait()
    finish_gather(X0)
    inv, pre = backward_inputs(0, X0)
    finish_gather(DY0)
    x_own, dy_own = backward(B0, 0, inv, pre)
    finish_gather(ACT0)
    act_own = forward(F0, 0)
    z_sum(B0)
    z_sum(F0)
    x_gather(X1)
    grad = input_grad(finish_sum(B0), x_own, dy_own).astype(bf16)
    hand_on(1, jnp.where(sec == 0, lines_of(loss_ref[0]), grad), prv, DY1)
    out = (act_own + finish_sum(F0)).astype(bf16)
    hand_on(0, jnp.where(sec == 7, lines_of(first_ref[0]), out), nxt, ACT1)
    put_pair(grad_ref, 0, grad.astype(f32))
    put_pair(out_ref, 0, out.astype(f32))

    wait_bytes(gat.at[DY1, 0, 0], pr.at[1])
    z_gather(DY1)
    wait_bytes(gat.at[ACT1, 0, 0], pr.at[0])
    z_gather(ACT1)
    finish_gather(X1)
    inv, pre = backward_inputs(1, X1)
    x_gather(DY1)
    x_gather(ACT1)
    finish_gather(DY1)
    x_own, dy_own = backward(B1, 1, inv, pre)

    for d in range(1, NX):
        pltpu.make_async_remote_copy(
            src_ref=gpart, dst_ref=gx.at[NX - d], send_sem=gs.at[0], recv_sem=gr.at[0],
            device_id=at_x(d), device_id_type=MESH,
        ).start()
    gx[0] = gpart[...]

    finish_gather(ACT1)
    act_own = forward(F1, 1)
    wait_bytes(gx.at[pl.ds(1, NX - 1)], gr.at[0])
    total = jnp.zeros((BLOCKS, 128), f32)
    for k in range(NX):
        total = total + gx[lax.rem(k - mx + NX, NX)]
    gz[0] = total

    def gain_send(d, _):
        pltpu.make_async_remote_copy(
            src_ref=gz.at[0], dst_ref=gz.at[NZ - d], send_sem=gs.at[1], recv_sem=gr.at[1],
            device_id=at_z(d), device_id_type=MESH,
        ).start()
        return 0

    z_sum(B1)
    lax.fori_loop(1, NZ, gain_send, 0)
    z_sum(F1)

    for c in range(0, BLOCKS, 4):
        part_cols = slice(c * 128, (c + 4) * 128)
        both = jnp.concatenate([normed[0, :, part_cols], normed[1, :, part_cols]], axis=0)
        upg[:, part_cols] = (dot(dpre[...], both) * 0.5).astype(bf16)
        both = jnp.concatenate([dyb[0, :, part_cols], dyb[1, :, part_cols]], axis=0)
        downg[:, part_cols] = (dot(hid[...], both) * 0.5).astype(bf16)
    store_up = pltpu.make_async_copy(upg, upg_hbm.at[0], og_sem.at[0])
    store_down = pltpu.make_async_copy(downg, downg_hbm.at[0], og_sem.at[1])
    store_up.start()
    store_down.start()

    put_pair(grad_ref, 1, input_grad(finish_sum(B1), x_own, dy_own))
    put_pair(out_ref, 1, act_own + finish_sum(F1))
    wait_bytes(gz.at[pl.ds(1, NZ - 1)], gr.at[1])
    total = jnp.zeros((BLOCKS, 128), f32)
    for k in range(NZ):
        total = total + gz[lax.rem(k - mz + NZ, NZ)]
    for c in range(BLOCKS):
        gaing_ref[:, c * 128 : (c + 1) * 128] = total[c : c + 1, :]

    for a in range(6):
        wait_bytes(gat.at[a, 0, pl.ds(1, NZ - 1)], zs.at[a])
        wait_bytes(gat.at[a, pl.ds(1, NX - 1)], xsnd.at[a])
    for r in range(4):
        wait_bytes(part.at[r, pl.ds(1, NX - 1)], xsnd.at[6 + r])
        wait_bytes(wire.at[r, pl.ds(1, NZ - 1)], zs.at[6 + r])
    for k in range(2):
        wait_bytes(pas.at[k], ps.at[k])
    wait_bytes(gx.at[pl.ds(1, NX - 1)], gs.at[0])
    wait_bytes(gz.at[pl.ds(1, NZ - 1)], gs.at[1])
    store_up.wait()
    store_down.wait()


def on_device(*args):
    vmem = pl.BlockSpec(memory_space=pltpu.VMEM)
    anywhere = pl.BlockSpec(memory_space=pl.ANY)
    return pl.pallas_call(
        kernel,
        out_shape=(
            jax.ShapeDtypeStruct((2, 1, 2, WIDTH), bf16),
            jax.ShapeDtypeStruct((2, 1, 2, WIDTH), bf16),
            jax.ShapeDtypeStruct((1, UNITS, WIDTH), bf16),
            jax.ShapeDtypeStruct((1, UNITS, WIDTH), bf16),
            jax.ShapeDtypeStruct((1, WIDTH), f32),
        ),
        in_specs=[vmem] * 8 + [anywhere] * 2,
        out_specs=(vmem, vmem, anywhere, anywhere, vmem),
        scratch_shapes=[
            pltpu.VMEM((UNITS, WIDTH), bf16),
            pltpu.VMEM((UNITS, WIDTH), bf16),
            pltpu.VMEM((6, NX, NZ, LINES, 128), bf16),
            pltpu.VMEM((BLOCKS * ROWS, 128), f32),
            pltpu.VMEM((BLOCKS * ROWS, 128), f32),
            pltpu.VMEM((BLOCKS * ROWS, 128), f32),
            pltpu.VMEM((3, ROWS, WIDTH), bf16),
            pltpu.VMEM((2, ROWS, WIDTH), bf16),
            pltpu.VMEM((UNITS, 2 * ROWS), bf16),
            pltpu.VMEM((UNITS, 2 * ROWS), bf16),
            pltpu.VMEM((4, NX, BLOCKS, 32, 128), bf16),
            pltpu.VMEM((4, NX - 1, BLOCKS, 32, 128), bf16),
            pltpu.VMEM((4, BLOCKS * 32, 128), f32),
            pltpu.VMEM((4, NZ, LINES, 128), bf16),
            pltpu.VMEM((4, NZ, LINES, 128), bf16),
            pltpu.VMEM((2, LINES, 128), bf16),
            pltpu.VMEM((BLOCKS, 128), f32),
            pltpu.VMEM((NX, BLOCKS, 128), f32),
            pltpu.VMEM((NZ, BLOCKS, 128), f32),
            pltpu.VMEM((4, ROWS, ROWS), bf16),
            pltpu.VMEM((UNITS, WIDTH), bf16),
            pltpu.VMEM((UNITS, WIDTH), bf16),
            pltpu.SemaphoreType.DMA((2,)),
            pltpu.SemaphoreType.DMA((10,)),
            pltpu.SemaphoreType.DMA((10,)),
            pltpu.SemaphoreType.DMA((10,)),
            pltpu.SemaphoreType.DMA((10,)),
            pltpu.SemaphoreType.DMA((2,)),
            pltpu.SemaphoreType.DMA((2,)),
            pltpu.SemaphoreType.DMA((2,)),
            pltpu.SemaphoreType.DMA((2,)),
            pltpu.SemaphoreType.DMA((2,)),
        ],
        compiler_params=pltpu.CompilerParams(
            collective_id=0, has_side_effects=True, vmem_limit_bytes=56 * 1024 * 1024
        ),
    )(*args)


def solution(mesh):
    placed = (
        P("section", "peer", None),
        P(None, "peer", None),
        P(None, "section", "peer", None),
        P("section", "peer", None),
        P(None, "peer", None),
        P(),
        P(),
        P("section", None),
        P("section", "peer", None),
        P("section", "peer", None),
    )
    return jax.shard_map(
        on_device,
        mesh=mesh,
        in_specs=placed,
        out_specs=(
            P(None, "section", "peer", None),
            P(None, "section", "peer", None),
            P("section", "peer", None),
            P("section", "peer", None),
            P("section", None),
        ),
        check_vma=False,
    )
```

```python
import jax
import jax.numpy as jnp
from jax import lax
from jax.experimental import pallas as pl
from jax.experimental.pallas import tpu as pltpu
from jax.sharding import PartitionSpec as P

MESH = pl.DeviceIdType.MESH
EPS = 1e-05
NX, NZ = 4, 16
ROWS = 128
BLOCKS = 5
SLICE = BLOCKS * 128
WIDTH = NX * SLICE
LINES = 8 * BLOCKS
PAIR = 2 * BLOCKS
UNITS = 160
X0, DY0, ACT0, X1, ACT1, DY1 = range(6)
B0, F0, B1, F1 = range(4)
PRE_B0, DH_B0, PRE_F0, PRE_B1, DH_B1, PRE_F1 = range(6)
IN_B0, IN_F0, IN_B1, IN_F1 = range(4)
f32, bf16 = jnp.float32, jnp.bfloat16


def dot(a, b):
    return jnp.dot(a, b, preferred_element_type=f32)


def dot_t(a, b):
    return lax.dot_general(a, b, (((1,), (1,)), ((), ())), preferred_element_type=f32)


def t_dot(a, b):
    return lax.dot_general(a, b, (((0,), (0,)), ((), ())), preferred_element_type=f32)


def wait_bytes(ref, sem):
    pltpu.make_async_copy(ref, ref, sem).wait()


def kernel(
    act_ref, first_ref, stored_ref, pend_ref, loss_ref, fw_ref, bw_ref, gain_ref, up_hbm, down_hbm,
    out_ref, grad_ref, upg_hbm, downg_hbm, gaing_ref,
    wu, wd, msgf, msg_out, msg_in, lines, gat, nat, xs, xg, dyb, fs, wire, rin, fin,
    xown, xo, xi, sq, ag, mm, full, hid, dpre, gpart, gz, gx, pas, resf, ro, ri, hot, upg, downg,
    w_sem, ws, wr, ms, mr, zs, zr, zs2, zr2, xsn, xrc, sqs, sqr, ags, agr, mms, mmr, fus, fur, ps, pr, rs, rr,
    gs, gr, og_sem,
):
    sec = lax.axis_index("section")
    peer = lax.axis_index("peer")
    mx, mz = peer // NZ, lax.rem(peer, NZ)
    even = lax.rem(mz, 2) == 0

    def at_z(d):
        return (sec, mx * NZ + lax.rem(mz + (d + NZ), NZ))

    def at_x(d):
        return (sec, lax.rem(mx + d, NX) * NZ + mz)

    nxt = (lax.rem(sec + 1, 8), peer)
    prv = (lax.rem(sec + 7, 8), peer)

    def send(src, dst, ssem, rsem, dev):
        pltpu.make_async_remote_copy(
            src_ref=src, dst_ref=dst, send_sem=ssem, recv_sem=rsem, device_id=dev, device_id_type=MESH
        ).start()

    def slice_of(x):
        return pl.ds(pl.multiple_of(x * SLICE, 128), SLICE)

    def rel(x):
        return lax.rem(x - mx + NX, NX)

    barrier = pltpu.get_barrier_semaphore()
    greeted = [at_z(d) for d in (1, 2, 3, 4, -1, -2, -3, -4)] + [at_x(d) for d in (1, 2, 3)] + [nxt, prv]
    for other in greeted:
        pl.semaphore_signal(barrier, inc=1, device_id=other, device_id_type=MESH)

    own_up = pltpu.make_async_copy(up_hbm.at[0, :, slice_of(mx)], wu.at[0], w_sem.at[0])
    own_down = pltpu.make_async_copy(down_hbm.at[0, :, slice_of(mx)], wd.at[0], w_sem.at[1])
    own_up.start()
    own_down.start()

    pairs = [stored_ref[0, 0], pend_ref[0], act_ref[0], stored_ref[1, 0], first_ref[0], loss_ref[0]]
    for x in range(NX):
        msgf[x, pl.ds(56, 8), :] = jnp.zeros((8, 128), f32)
    for a, pair in enumerate(pairs):
        flat = pair.astype(f32)
        for x in range(NX):
            for c in range(BLOCKS):
                col = (x * BLOCKS + c) * 128
                msgf[x, pl.ds(a * PAIR + 2 * c, 2), :] = flat[:, col : col + 128]
    for x in range(NX):
        msg_out[x] = msgf[x].astype(bf16)
    pl.semaphore_wait(barrier, len(greeted))

    for d in (2, 1, 3):
        send(msg_out.at[lax.rem(mx + d, NX)], msg_in.at[NX - d], ms.at[0], mr.at[0], at_x(d))
    for k, (src, dst) in enumerate(((up_hbm, wu), (down_hbm, wd))):
        for d in (2, 1, 3):
            send(src.at[0, :, slice_of(lax.rem(mx + d, NX))], dst.at[NX - d], ws.at[k], wr.at[k], at_x(d))
    msg_in[0] = msg_out[mx]
    wait_bytes(msg_in.at[pl.ds(1, NX - 1)], mr.at[0])
    for x in range(NX):
        got = msg_in[rel(x)].astype(f32)
        for a in range(6):
            for c in range(BLOCKS):
                lines[a, pl.ds(8 * c + 2 * x, 2), :] = got[a * PAIR + 2 * c : a * PAIR + 2 * c + 2, :]

    def z_first(buf, ssem, rsem):
        send(buf.at[0], buf.at[12], ssem, rsem.at[0], at_z(4))
        send(buf.at[0], buf.at[4], ssem, rsem.at[1], at_z(-4))
        for d in (3, 2, 1):
            send(buf.at[0], buf.at[NZ - d], ssem, rsem.at[2], at_z(d))
            send(buf.at[0], buf.at[d], ssem, rsem.at[3], at_z(-d))

    def z_relay(buf, ssem, rsem):
        wait_bytes(buf.at[12], rsem.at[0])
        wait_bytes(buf.at[4], rsem.at[1])
        send(buf.at[jnp.where(even, 12, 4)], buf.at[8], ssem, rsem.at[4], at_z(jnp.where(even, 4, -4)))
        for d in (3, 2, 1):
            send(buf.at[12], buf.at[12 - d], ssem, rsem.at[5], at_z(d))
            send(buf.at[4], buf.at[4 + d], ssem, rsem.at[6], at_z(-d))

    def z_done(buf, rsem):
        wait_bytes(buf.at[pl.ds(13, 3)], rsem.at[2])
        wait_bytes(buf.at[pl.ds(1, 3)], rsem.at[3])
        wait_bytes(buf.at[8], rsem.at[4])
        wait_bytes(buf.at[pl.ds(9, 3)], rsem.at[5])
        wait_bytes(buf.at[pl.ds(5, 3)], rsem.at[6])

    def gather_first(a):
        z_first(gat.at[a], zs.at[a], zr.at[a])

    def gather_relay(a):
        z_relay(gat.at[a], zs.at[a], zr.at[a])

    for a in (X0, DY0, ACT0, X1):
        gat[a, 0] = lines[a].astype(bf16)
    gather_first(X0)
    gather_first(DY0)
    gather_first(ACT0)

    def sum_first(r):
        def fill(k):
            wire[r, k] = fs[r, pl.ds(k, LINES, stride=NZ), :].astype(bf16)

        for k in (8, 7, 9, 6, 10, 5, 11):
            fill(k)
        send(wire.at[r, 8], rin.at[r, 6], zs2.at[r], zr2.at[r, 0], at_z(jnp.where(even, 4, -4)))
        for d in (3, 2, 1):
            send(wire.at[r, 4 + d], rin.at[r, d - 1], zs2.at[r], zr2.at[r, 0], at_z(d))
            send(wire.at[r, 12 - d], rin.at[r, 2 + d], zs2.at[r], zr2.at[r, 0], at_z(-d))
        for d in (3, 2, 1):
            fill(d)
            fill(NZ - d)
            send(wire.at[r, d], fin.at[r, d - 1], zs2.at[r], zr2.at[r, 1], at_z(d))
            send(wire.at[r, NZ - d], fin.at[r, 2 + d], zs2.at[r], zr2.at[r, 1], at_z(-d))

    def sum_relay(r):
        ahead = fs[r, pl.ds(4, LINES, stride=NZ), :]
        behind = fs[r, pl.ds(12, LINES, stride=NZ), :]
        wait_bytes(rin.at[r], zr2.at[r, 0])
        across = rin[r, 6].astype(f32)
        for k in range(3):
            ahead = ahead + rin[r, k].astype(f32)
            behind = behind + rin[r, 3 + k].astype(f32)
        wire[r, 4] = (ahead + jnp.where(even, across, 0.0)).astype(bf16)
        wire[r, 12] = (behind + jnp.where(even, 0.0, across)).astype(bf16)
        send(wire.at[r, 4], fin.at[r, 6], zs2.at[r], zr2.at[r, 1], at_z(4))
        send(wire.at[r, 12], fin.at[r, 7], zs2.at[r], zr2.at[r, 1], at_z(-4))

    def sum_done(r):
        total = fs[r, pl.ds(0, LINES, stride=NZ), :]
        wait_bytes(fin.at[r], zr2.at[r, 1])
        for k in range(8):
            total = total + fin[r, k].astype(f32)
        return total

    def row_of(index):
        group = index // NZ
        return 2 * ((group // 2) * NZ + lax.rem(mz + lax.rem(index, NZ), NZ)) + lax.rem(group, 2)

    lane = lax.broadcasted_iota(jnp.int32, (ROWS, ROWS), 1)
    placed = row_of(lax.broadcasted_iota(jnp.int32, (ROWS, ROWS), 0)) == lane
    lane_row = row_of(lane).astype(f32)

    def one_hot(route):
        picked = jnp.sum(jnp.where(placed, route.astype(f32), 0.0), axis=1, keepdims=True)
        return jnp.where(picked == lane_row, 1.0, 0.0)

    for tick in range(2):
        hot[tick] = one_hot(fw_ref[tick, pl.ds(sec, 1), :]).astype(bf16)
        hot[2 + tick] = one_hot(bw_ref[tick, pl.ds(sec, 1), :]).T.astype(bf16)

    gain = gain_ref[:, slice_of(mx)]
    gain_of = [gain[:, c * 128 : (c + 1) * 128] for c in range(BLOCKS)]

    def block(c):
        return slice(c * 128, (c + 1) * 128)

    def turned(a, index):
        z_done(gat.at[a], zr.at[a])
        for k in range(NZ):
            nat[pl.ds(k, LINES, stride=NZ), :] = gat[a, k].astype(f32)
        both = jnp.concatenate([nat[pl.ds(c * 128, 128), :] for c in range(BLOCKS)], axis=1)
        return dot(hot[index], both.astype(bf16))

    def take_input(a, e, index):
        got = turned(a, index)
        total = jnp.zeros((ROWS, 128), f32)
        for c in range(BLOCKS):
            part = got[:, block(c)]
            xs[e, pl.ds(c * 128, 128), :] = part
            xg[e, :, block(c)] = (part * gain_of[c]).astype(bf16)
            total = total + part * part
        sq[e, 0] = jnp.broadcast_to(jnp.sum(total.T, axis=0, keepdims=True), (8, 128))
        for d in (2, 1, 3):
            send(sq.at[e, 0], sq.at[e, NX - d], sqs.at[e], sqr.at[e], at_x(d))

    def take_grad(a, tick, index):
        got = turned(a, index)
        dyb[tick] = got.astype(bf16)
        own = [got[0:1, :]]
        for c in range(BLOCKS):
            lines[tick, pl.ds(8 * c, 8), :] = jnp.concatenate(
                [got[16 * k : 16 * k + 1, block(c)] for k in range(8)], axis=0
            )

    def x_parts(e, weight, rows):
        for d in (2, 1, 3):
            xo[e, d] = dot_t(weight[d], rows).astype(bf16)
            send(xo.at[e, d], xi.at[e, NX - d], xsn.at[e], xrc.at[e], at_x(d))
        xown[e] = dot_t(weight[0], rows)

    def x_total(e):
        wait_bytes(xi.at[e, pl.ds(1, NX - 1)], xrc.at[e])
        total = xown[e]
        for k in range(1, NX):
            total = total + xi[e, k].astype(f32)
        return total

    def x_gather(g, value):
        ag[g, 0] = value
        for d in (2, 1, 3):
            send(ag.at[g, 0], ag.at[g, NX - d], ags.at[g], agr.at[g], at_x(d))

    def x_gathered(g):
        wait_bytes(ag.at[g, pl.ds(1, NX - 1)], agr.at[g])
        return ag[g].reshape(NX * UNITS, ROWS)

    def inv_rms(e):
        wait_bytes(sq.at[e, pl.ds(1, NX - 1)], sqr.at[e])
        total = sq[e, 0] + sq[e, 1] + sq[e, 2] + sq[e, 3]
        return lax.rsqrt(total[0:1, :] * (1.0 / WIDTH) + EPS)

    def by_row(value):
        return jnp.broadcast_to(value, (ROWS, ROWS)).T

    def spread_full(n, value):
        for c in range(BLOCKS):
            full[n, 0, :, block(c)] = value(c)
        for d in (2, 1, 3):
            send(full.at[n, 0], full.at[n, NX - d], fus.at[n], fur.at[n], at_x(d))

    def normed_block(e, inv_rows):
        return lambda c: (xs[e, pl.ds(c * 128, 128), :] * inv_rows * gain_of[c]).astype(bf16)

    def own_lines(ref):
        return ref[pl.ds(0, LINES, stride=NZ), :]

    def hidden_forward(e, pre_e, g):
        pre = x_total(pre_e) * inv_rms(e)
        x_gather(g, (pre / (1.0 + jnp.exp(-pre))).astype(bf16))

    def branch_forward(r, g):
        branch = t_dot(x_gathered(g), wd[...].reshape(NX * UNITS, SLICE))
        for c in range(BLOCKS):
            fs[r, pl.ds(c * 128, 128), :] = branch[:, block(c)]
        sum_first(r)

    def pre_backward(e, pre_e, tick):
        inv = inv_rms(e)
        pre = x_total(pre_e) * inv
        sig = 1.0 / (1.0 + jnp.exp(-pre))
        hid[:, tick * ROWS : (tick + 1) * ROWS] = (pre * sig).astype(bf16)
        return inv, pre, sig * (1.0 + pre * (1.0 - sig))

    def d_pre_backward(tick, dh_e, g, pre, slope):
        d_pre = (x_total(dh_e) * slope).astype(bf16)
        x_gather(g, d_pre)
        dpre[:, tick * ROWS : (tick + 1) * ROWS] = d_pre
        mm[tick, 0] = jnp.broadcast_to(jnp.sum(d_pre.astype(f32) * pre, axis=0, keepdims=True), (8, 128))
        for d in (2, 1, 3):
            send(mm.at[tick, 0], mm.at[tick, NX - d], mms.at[tick], mmr.at[tick], at_x(d))

    def branch_backward(r, g, e, tick, inv, inv_rows):
        d_norm = t_dot(x_gathered(g), wu[...].reshape(NX * UNITS, SLICE))
        wait_bytes(mm.at[tick, pl.ds(1, NX - 1)], mmr.at[tick])
        total = (mm[tick, 0] + mm[tick, 1] + mm[tick, 2] + mm[tick, 3])[0:1, :]
        back = by_row(total * inv * inv * (1.0 / WIDTH))
        for c in range(BLOCKS):
            x = xs[e, pl.ds(c * 128, 128), :]
            part = d_norm[:, block(c)] * inv_rows
            fs[r, pl.ds(c * 128, 128), :] = part * gain_of[c] - x * back
            line = jnp.sum(part * x, axis=0, keepdims=True)
            if tick == 0:
                gpart[c : c + 1, :] = line
            else:
                gpart[c : c + 1, :] += line
        sum_first(r)

    def hand_on(k, value, other, a):
        pas[k] = value
        send(pas.at[k], gat.at[a, 0], ps.at[k], pr.at[k], other)

    def results_out(q, value):
        resf[q] = value
        for x in range(NX):
            ro[q, x] = jnp.concatenate(
                [resf[q, pl.ds(8 * c + 2 * x, 2), :] for c in range(BLOCKS)] + [jnp.zeros((6, 128), f32)], axis=0
            ).astype(bf16)
        for d in (2, 1, 3):
            send(ro.at[q, lax.rem(mx + d, NX)], ri.at[q, NX - d], rs.at[q], rr.at[q], at_x(d))
        ri[q, 0] = ro[q, mx]

    def results_in(q, ref, tick):
        wait_bytes(ri.at[q, pl.ds(1, NX - 1)], rr.at[q])
        for x in range(NX):
            got = ri[q, rel(x)].astype(f32)
            for c in range(BLOCKS):
                col = (x * BLOCKS + c) * 128
                ref[tick, 0, :, col : col + 128] = got[2 * c : 2 * c + 2, :].astype(bf16)

    first_lines = lines[4].astype(bf16)
    loss_lines = lines[5].astype(bf16)
    gather_relay(X0)
    gather_relay(DY0)
    gather_relay(ACT0)
    gather_first(X1)
    take_input(X0, IN_B0, 2)
    own_up.wait()
    wait_bytes(wu.at[pl.ds(1, NX - 1)], wr.at[0])
    x_parts(PRE_B0, wu, xg[IN_B0])
    take_grad(DY0, 0, 2)
    own_down.wait()
    wait_bytes(wd.at[pl.ds(1, NX - 1)], wr.at[1])
    x_parts(DH_B0, wd, dyb[0])
    take_input(ACT0, IN_F0, 0)
    x_parts(PRE_F0, wu, xg[IN_F0])
    gather_relay(X1)
    inv, pre, slope = pre_backward(IN_B0, PRE_B0, 0)
    d_pre_backward(0, DH_B0, 0, pre, slope)
    hidden_forward(IN_F0, PRE_F0, 1)
    inv_rows = by_row(inv)
    branch_backward(B0, 0, IN_B0, 0, inv, inv_rows)
    branch_forward(F0, 1)
    spread_full(0, normed_block(IN_B0, inv_rows))
    sum_relay(B0)
    sum_relay(F0)
    spread_full(1, lambda c: dyb[0, :, block(c)])
    grad = (sum_done(B0) + lines[0]).astype(bf16)
    hand_on(1, jnp.where(sec == 0, loss_lines, grad), prv, DY1)
    out = (sum_done(F0) + own_lines(xs.at[IN_F0])).astype(bf16)
    hand_on(0, jnp.where(sec == 7, first_lines, out), nxt, ACT1)
    take_input(X1, IN_B1, 3)
    x_parts(PRE_B1, wu, xg[IN_B1])

    wait_bytes(gat.at[DY1, 0], pr.at[1])
    gather_first(DY1)
    wait_bytes(gat.at[ACT1, 0], pr.at[0])
    gather_first(ACT1)
    results_out(0, out.astype(f32))
    results_out(1, grad.astype(f32))
    inv, pre, slope = pre_backward(IN_B1, PRE_B1, 1)
    inv_rows = by_row(inv)
    gather_relay(DY1)
    gather_relay(ACT1)
    spread_full(2, normed_block(IN_B1, inv_rows))
    take_grad(DY1, 1, 3)
    x_parts(DH_B1, wd, dyb[1])
    take_input(ACT1, IN_F1, 1)
    x_parts(PRE_F1, wu, xg[IN_F1])
    d_pre_backward(1, DH_B1, 2, pre, slope)
    hidden_forward(IN_F1, PRE_F1, 3)
    spread_full(3, lambda c: dyb[1, :, block(c)])
    branch_backward(B1, 2, IN_B1, 1, inv, inv_rows)
    branch_forward(F1, 3)
    gz[0] = jnp.concatenate([gpart[...], jnp.zeros((8 - BLOCKS, 128), f32)], axis=0)
    z_first(gz, gs.at[0], gr)
    sum_relay(B1)
    sum_relay(F1)
    z_relay(gz, gs.at[0], gr)
    results_in(0, out_ref, 0)
    results_in(1, grad_ref, 0)

    for n in range(4):
        wait_bytes(full.at[n, pl.ds(1, NX - 1)], fur.at[n])
    stores = []
    for x in range(NX):
        where = slice_of(lax.rem(mx + x, NX))
        for k, (left, at, grads, hbm) in enumerate(((dpre, 0, upg, upg_hbm), (hid, 1, downg, downg_hbm))):
            both = jnp.concatenate([full[at, x], full[2 + at, x]], axis=0)
            grads[x] = (dot(left[...], both) * 0.5).astype(bf16)
            store = pltpu.make_async_copy(grads.at[x], hbm.at[0, :, where], og_sem.at[k, x])
            store.start()
            stores.append(store)

    results_out(2, sum_done(B1) + lines[1])
    results_out(3, sum_done(F1) + own_lines(xs.at[IN_F1]))
    z_done(gz, gr)
    total = jnp.zeros((8, 128), f32)
    for z in range(NZ):
        total = total + gz[lax.rem(z - mz + NZ, NZ)]
    gx[0] = total
    for d in (2, 1, 3):
        send(gx.at[0], gx.at[NX - d], gs.at[1], gr.at[7], at_x(d))
    results_in(2, grad_ref, 1)
    results_in(3, out_ref, 1)
    wait_bytes(gx.at[pl.ds(1, NX - 1)], gr.at[7])
    for x in range(NX):
        got = gx[rel(x)]
        for c in range(BLOCKS):
            col = (x * BLOCKS + c) * 128
            gaing_ref[:, col : col + 128] = got[c : c + 1, :]

    three = pl.ds(1, NX - 1)
    wait_bytes(msg_in.at[three], ms.at[0])
    wait_bytes(wu.at[three], ws.at[0])
    wait_bytes(wd.at[three], ws.at[1])
    for a in range(6):
        wait_bytes(gat.at[a, pl.ds(1, NZ - 1)], zs.at[a])
        wait_bytes(xi.at[a, three], xsn.at[a])
    for r in range(4):
        wait_bytes(wire.at[r, pl.ds(1, NZ - 1)], zs2.at[r])
        wait_bytes(sq.at[r, three], sqs.at[r])
        wait_bytes(ag.at[r, three], ags.at[r])
        wait_bytes(full.at[r, three], fus.at[r])
        wait_bytes(ri.at[r, three], rs.at[r])
    for k in range(2):
        wait_bytes(mm.at[k, three], mms.at[k])
        wait_bytes(pas.at[k], ps.at[k])
    wait_bytes(gz.at[pl.ds(1, NZ - 1)], gs.at[0])
    wait_bytes(gx.at[three], gs.at[1])
    for store in stores:
        store.wait()


def on_device(*args):
    vmem = pl.BlockSpec(memory_space=pltpu.VMEM)
    anywhere = pl.BlockSpec(memory_space=pl.ANY)
    dma = pltpu.SemaphoreType.DMA
    shapes = (
        jax.ShapeDtypeStruct((2, 1, 2, WIDTH), bf16),
        jax.ShapeDtypeStruct((2, 1, 2, WIDTH), bf16),
        jax.ShapeDtypeStruct((1, UNITS, WIDTH), bf16),
        jax.ShapeDtypeStruct((1, UNITS, WIDTH), bf16),
        jax.ShapeDtypeStruct((1, WIDTH), f32),
    )
    return pl.pallas_call(
        kernel,
        out_shape=shapes,
        in_specs=[vmem] * 8 + [anywhere] * 2,
        out_specs=(vmem, vmem, anywhere, anywhere, vmem),
        scratch_shapes=[
            pltpu.VMEM((NX, UNITS, SLICE), bf16),
            pltpu.VMEM((NX, UNITS, SLICE), bf16),
            pltpu.VMEM((NX, 64, 128), f32),
            pltpu.VMEM((NX, 64, 128), bf16),
            pltpu.VMEM((NX, 64, 128), bf16),
            pltpu.VMEM((6, LINES, 128), f32),
            pltpu.VMEM((6, NZ, LINES, 128), bf16),
            pltpu.VMEM((SLICE, 128), f32),
            pltpu.VMEM((4, SLICE, 128), f32),
            pltpu.VMEM((4, ROWS, SLICE), bf16),
            pltpu.VMEM((2, ROWS, SLICE), bf16),
            pltpu.VMEM((4, SLICE, 128), f32),
            pltpu.VMEM((4, NZ, LINES, 128), bf16),
            pltpu.VMEM((4, 7, LINES, 128), bf16),
            pltpu.VMEM((4, 8, LINES, 128), bf16),
            pltpu.VMEM((6, UNITS, ROWS), f32),
            pltpu.VMEM((6, NX, UNITS, ROWS), bf16),
            pltpu.VMEM((6, NX, UNITS, ROWS), bf16),
            pltpu.VMEM((4, NX, 8, 128), f32),
            pltpu.VMEM((4, NX, UNITS, ROWS), bf16),
            pltpu.VMEM((2, NX, 8, 128), f32),
            pltpu.VMEM((4, NX, ROWS, SLICE), bf16),
            pltpu.VMEM((UNITS, 2 * ROWS), bf16),
            pltpu.VMEM((UNITS, 2 * ROWS), bf16),
            pltpu.VMEM((BLOCKS, 128), f32),
            pltpu.VMEM((NZ, 8, 128), f32),
            pltpu.VMEM((NX, 8, 128), f32),
            pltpu.VMEM((2, LINES, 128), bf16),
            pltpu.VMEM((4, LINES, 128), f32),
            pltpu.VMEM((4, NX, 16, 128), bf16),
            pltpu.VMEM((4, NX, 16, 128), bf16),
            pltpu.VMEM((4, ROWS, ROWS), bf16),
            pltpu.VMEM((NX, UNITS, SLICE), bf16),
            pltpu.VMEM((NX, UNITS, SLICE), bf16),
            dma((2,)),
            dma((2,)),
            dma((2,)),
            dma((1,)),
            dma((1,)),
            dma((6,)),
            dma((6, 7)),
            dma((4,)),
            dma((4, 2)),
            dma((6,)),
            dma((6,)),
            dma((4,)),
            dma((4,)),
            dma((4,)),
            dma((4,)),
            dma((2,)),
            dma((2,)),
            dma((4,)),
            dma((4,)),
            dma((2,)),
            dma((2,)),
            dma((4,)),
            dma((4,)),
            dma((2,)),
            dma((8,)),
            dma((2, NX)),
        ],
        compiler_params=pltpu.CompilerParams(
            collective_id=0, has_side_effects=True, vmem_limit_bytes=56 * 1024 * 1024
        ),
    )(*args)


def solution(mesh):
    placed = (
        P("section", "peer", None),
        P(None, "peer", None),
        P(None, "section", "peer", None),
        P("section", "peer", None),
        P(None, "peer", None),
        P(),
        P(),
        P("section", None),
        P("section", "peer", None),
        P("section", "peer", None),
    )
    return jax.shard_map(
        on_device,
        mesh=mesh,
        in_specs=placed,
        out_specs=(
            P(None, "section", "peer", None),
            P(None, "section", "peer", None),
            P("section", "peer", None),
            P("section", "peer", None),
            P("section", None),
        ),
        check_vma=False,
    )
```

```python
import jax
import jax.numpy as jnp
from jax import lax
from jax.experimental import pallas as pl
from jax.experimental.pallas import tpu as pltpu
from jax.sharding import PartitionSpec as P

MESH = pl.DeviceIdType.MESH
EPS = 1e-05
NX, NZ = 4, 16
ROWS = 128
BLOCKS = 5
SLICE = BLOCKS * 128
WIDTH = NX * SLICE
LINES = 8 * BLOCKS
PAIR = 2 * BLOCKS
UNITS = 160
X0, DY0, ACT0, X1, ACT1, DY1 = range(6)
B0, F0, B1, F1 = range(4)
PRE_B0, DH_B0, PRE_F0, PRE_B1, DH_B1, PRE_F1 = range(6)
IN_B0, IN_F0, IN_B1, IN_F1 = range(4)
f32, bf16 = jnp.float32, jnp.bfloat16


def dot(a, b):
    return jnp.dot(a, b, preferred_element_type=f32)


def dot_t(a, b):
    return lax.dot_general(a, b, (((1,), (1,)), ((), ())), preferred_element_type=f32)


def t_dot(a, b):
    return lax.dot_general(a, b, (((0,), (0,)), ((), ())), preferred_element_type=f32)


def wait_bytes(ref, sem):
    pltpu.make_async_copy(ref, ref, sem).wait()


def kernel(
    act_ref, first_ref, stored_ref, pend_ref, loss_ref, fw_ref, bw_ref, gain_ref, up_hbm, down_hbm,
    out_ref, grad_ref, upg_hbm, downg_hbm, gaing_ref,
    wu, wd, msgf, msg_out, msg_in, lines, gat, nat, xs, xg, dyb, fs, wire, rin, fin,
    xown, xo, xi, sq, ag, mm, full, hid, dpre, gpart, gz, gx, pas, resf, ro, ri, hot, upg, downg,
    w_sem, ws, wr, ms, mr, zs, zr, zs2, zr2, xsn, xrc, sqs, sqr, ags, agr, mms, mmr, fus, fur, ps, pr, rs, rr,
    gs, gr, og_sem, ready,
):
    sec = lax.axis_index("section")
    peer = lax.axis_index("peer")
    mx, mz = peer // NZ, lax.rem(peer, NZ)
    even = lax.rem(mz, 2) == 0

    after, before = lax.rem(sec + 1, 8), lax.rem(sec + 7, 8)

    def at_z(d, section=sec):
        return (section, mx * NZ + lax.rem(mz + (d + NZ), NZ))

    def at_x(d):
        return (sec, lax.rem(mx + d, NX) * NZ + mz)

    def send(src, dst, ssem, rsem, dev):
        pltpu.make_async_remote_copy(
            src_ref=src, dst_ref=dst, send_sem=ssem, recv_sem=rsem, device_id=dev, device_id_type=MESH
        ).start()

    def slice_of(x):
        return pl.ds(pl.multiple_of(x * SLICE, 128), SLICE)

    def rel(x):
        return lax.rem(x - mx + NX, NX)

    barrier = pltpu.get_barrier_semaphore()
    steps = (1, 2, 3, 4, -1, -2, -3, -4)
    greeted = [at_z(d) for d in steps] + [at_x(d) for d in (1, 2, 3)] + [at_z(0, after), at_z(0, before)]
    for other in greeted:
        pl.semaphore_signal(barrier, inc=1, device_id=other, device_id_type=MESH)

    own_up = pltpu.make_async_copy(up_hbm.at[0, :, slice_of(mx)], wu.at[0], w_sem.at[0])
    own_down = pltpu.make_async_copy(down_hbm.at[0, :, slice_of(mx)], wd.at[0], w_sem.at[1])
    own_up.start()
    own_down.start()

    pairs = [stored_ref[0, 0], pend_ref[0], act_ref[0], stored_ref[1, 0], first_ref[0], loss_ref[0]]
    for x in range(NX):
        msgf[x, pl.ds(56, 8), :] = jnp.zeros((8, 128), f32)
    for a, pair in enumerate(pairs):
        flat = pair.astype(f32)
        for x in range(NX):
            for c in range(BLOCKS):
                col = (x * BLOCKS + c) * 128
                msgf[x, pl.ds(a * PAIR + 2 * c, 2), :] = flat[:, col : col + 128]
    for x in range(NX):
        msg_out[x] = msgf[x].astype(bf16)
    pl.semaphore_wait(barrier, len(greeted))
    pl.semaphore_signal(ready.at[0], inc=1, device_id=at_z(0, before), device_id_type=MESH)
    pl.semaphore_signal(ready.at[1], inc=1, device_id=at_z(0, after), device_id_type=MESH)

    for d in (2, 1, 3):
        send(msg_out.at[lax.rem(mx + d, NX)], msg_in.at[NX - d], ms.at[0], mr.at[0], at_x(d))
    for k, (src, dst) in enumerate(((up_hbm, wu), (down_hbm, wd))):
        for d in (2, 1, 3):
            send(src.at[0, :, slice_of(lax.rem(mx + d, NX))], dst.at[NX - d], ws.at[k], wr.at[k], at_x(d))
    msg_in[0] = msg_out[mx]
    wait_bytes(msg_in.at[pl.ds(1, NX - 1)], mr.at[0])
    for x in range(NX):
        got = msg_in[rel(x)].astype(f32)
        for a in range(6):
            for c in range(BLOCKS):
                lines[a, pl.ds(8 * c + 2 * x, 2), :] = got[a * PAIR + 2 * c : a * PAIR + 2 * c + 2, :]

    def z_first(src, buf, ssem, rsem, section=sec):
        send(src, buf.at[12], ssem, rsem.at[0], at_z(4, section))
        send(src, buf.at[4], ssem, rsem.at[1], at_z(-4, section))
        for d in (3, 2, 1):
            send(src, buf.at[NZ - d], ssem, rsem.at[2], at_z(d, section))
            send(src, buf.at[d], ssem, rsem.at[3], at_z(-d, section))

    def z_relay(buf, ssem, rsem):
        wait_bytes(buf.at[12], rsem.at[0])
        wait_bytes(buf.at[4], rsem.at[1])
        send(buf.at[jnp.where(even, 12, 4)], buf.at[8], ssem, rsem.at[4], at_z(jnp.where(even, 4, -4)))
        for d in (3, 2, 1):
            send(buf.at[12], buf.at[12 - d], ssem, rsem.at[5], at_z(d))
            send(buf.at[4], buf.at[4 + d], ssem, rsem.at[6], at_z(-d))

    def z_near(buf, rsem):
        wait_bytes(buf.at[pl.ds(13, 3)], rsem.at[2])
        wait_bytes(buf.at[pl.ds(1, 3)], rsem.at[3])

    def z_far(buf, rsem):
        wait_bytes(buf.at[8], rsem.at[4])
        wait_bytes(buf.at[pl.ds(9, 3)], rsem.at[5])
        wait_bytes(buf.at[pl.ds(5, 3)], rsem.at[6])

    def gather_first(a):
        z_first(gat.at[a, 0], gat.at[a], zs.at[a], zr.at[a])

    def gather_relay(a):
        z_relay(gat.at[a], zs.at[a], zr.at[a])

    for a in (X0, DY0, ACT0, X1):
        gat[a, 0] = lines[a].astype(bf16)
    gather_first(ACT0)
    gather_first(X0)
    gather_first(DY0)

    def sum_first(r):
        def fill(k):
            wire[r, k] = fs[r, pl.ds(k, LINES, stride=NZ), :].astype(bf16)

        for k in (8, 7, 9, 6, 10, 5, 11):
            fill(k)
        send(wire.at[r, 8], rin.at[r, 6], zs2.at[r], zr2.at[r, 0], at_z(jnp.where(even, 4, -4)))
        for d in (3, 2, 1):
            send(wire.at[r, 4 + d], rin.at[r, d - 1], zs2.at[r], zr2.at[r, 0], at_z(d))
            send(wire.at[r, 12 - d], rin.at[r, 2 + d], zs2.at[r], zr2.at[r, 0], at_z(-d))
        for d in (3, 2, 1):
            fill(d)
            fill(NZ - d)
            send(wire.at[r, d], fin.at[r, d - 1], zs2.at[r], zr2.at[r, 1], at_z(d))
            send(wire.at[r, NZ - d], fin.at[r, 2 + d], zs2.at[r], zr2.at[r, 1], at_z(-d))

    def sum_relay(r):
        ahead = fs[r, pl.ds(4, LINES, stride=NZ), :]
        behind = fs[r, pl.ds(12, LINES, stride=NZ), :]
        wait_bytes(rin.at[r], zr2.at[r, 0])
        across = rin[r, 6].astype(f32)
        for k in range(3):
            ahead = ahead + rin[r, k].astype(f32)
            behind = behind + rin[r, 3 + k].astype(f32)
        wire[r, 4] = (ahead + jnp.where(even, across, 0.0)).astype(bf16)
        wire[r, 12] = (behind + jnp.where(even, 0.0, across)).astype(bf16)
        send(wire.at[r, 4], fin.at[r, 6], zs2.at[r], zr2.at[r, 1], at_z(4))
        send(wire.at[r, 12], fin.at[r, 7], zs2.at[r], zr2.at[r, 1], at_z(-4))

    def sum_done(r):
        total = fs[r, pl.ds(0, LINES, stride=NZ), :]
        wait_bytes(fin.at[r], zr2.at[r, 1])
        for k in range(8):
            total = total + fin[r, k].astype(f32)
        return total

    def row_of(index):
        group = index // NZ
        return 2 * ((group // 2) * NZ + lax.rem(mz + lax.rem(index, NZ), NZ)) + lax.rem(group, 2)

    lane = lax.broadcasted_iota(jnp.int32, (ROWS, ROWS), 1)
    placed = row_of(lax.broadcasted_iota(jnp.int32, (ROWS, ROWS), 0)) == lane
    lane_row = row_of(lane).astype(f32)

    def one_hot(route):
        picked = jnp.sum(jnp.where(placed, route.astype(f32), 0.0), axis=1, keepdims=True)
        return jnp.where(picked == lane_row, 1.0, 0.0)

    for tick in range(2):
        hot[tick] = one_hot(fw_ref[tick, pl.ds(sec, 1), :]).astype(bf16)
        hot[2 + tick] = one_hot(bw_ref[tick, pl.ds(sec, 1), :]).T.astype(bf16)

    gain = gain_ref[:, slice_of(mx)]
    gain_of = [gain[:, c * 128 : (c + 1) * 128] for c in range(BLOCKS)]

    def block(c):
        return slice(c * 128, (c + 1) * 128)

    def turned(a, index):
        z_near(gat.at[a], zr.at[a])
        for k in (0, 1, 2, 3, 4, 12, 13, 14, 15):
            nat[pl.ds(k, LINES, stride=NZ), :] = gat[a, k].astype(f32)
        z_far(gat.at[a], zr.at[a])
        for k in range(5, 12):
            nat[pl.ds(k, LINES, stride=NZ), :] = gat[a, k].astype(f32)
        both = jnp.concatenate([nat[pl.ds(c * 128, 128), :] for c in range(BLOCKS)], axis=1)
        return dot(hot[index], both.astype(bf16))

    def take_input(a, e, index):
        got = turned(a, index)
        total = jnp.zeros((ROWS, 128), f32)
        for c in range(BLOCKS):
            part = got[:, block(c)]
            xs[e, pl.ds(c * 128, 128), :] = part
            xg[e, :, block(c)] = (part * gain_of[c]).astype(bf16)
            total = total + part * part
        sq[e, 0] = jnp.broadcast_to(jnp.sum(total.T, axis=0, keepdims=True), (8, 128))
        for d in (2, 1, 3):
            send(sq.at[e, 0], sq.at[e, NX - d], sqs.at[e], sqr.at[e], at_x(d))

    def take_grad(a, tick, index):
        got = turned(a, index)
        dyb[tick] = got.astype(bf16)
        for c in range(BLOCKS):
            lines[tick, pl.ds(8 * c, 8), :] = jnp.concatenate(
                [got[16 * k : 16 * k + 1, block(c)] for k in range(8)], axis=0
            )

    def x_parts(e, weight, rows):
        parts = dot_t(weight[...].reshape(NX * UNITS, SLICE), rows)
        for d in (2, 1, 3):
            xo[e, d] = parts[d * UNITS : (d + 1) * UNITS, :].astype(bf16)
            send(xo.at[e, d], xi.at[e, NX - d], xsn.at[e], xrc.at[e], at_x(d))
        xown[e] = parts[:UNITS, :]

    def x_total(e):
        wait_bytes(xi.at[e, pl.ds(1, NX - 1)], xrc.at[e])
        total = xown[e]
        for k in range(1, NX):
            total = total + xi[e, k].astype(f32)
        return total

    def x_gather(g, value):
        ag[g, 0] = value
        for d in (2, 1, 3):
            send(ag.at[g, 0], ag.at[g, NX - d], ags.at[g], agr.at[g], at_x(d))

    def x_gathered(g):
        wait_bytes(ag.at[g, pl.ds(1, NX - 1)], agr.at[g])
        return ag[g].reshape(NX * UNITS, ROWS)

    def inv_rms(e):
        wait_bytes(sq.at[e, pl.ds(1, NX - 1)], sqr.at[e])
        total = sq[e, 0] + sq[e, 1] + sq[e, 2] + sq[e, 3]
        return lax.rsqrt(total[0:1, :] * (1.0 / WIDTH) + EPS)

    def by_row(value):
        return jnp.broadcast_to(value, (ROWS, ROWS)).T

    def spread_full(n, value):
        for c in range(BLOCKS):
            full[n, 0, :, block(c)] = value(c)
        for d in (2, 1, 3):
            send(full.at[n, 0], full.at[n, NX - d], fus.at[n], fur.at[n], at_x(d))

    def normed_block(e, inv_rows):
        return lambda c: (xs[e, pl.ds(c * 128, 128), :] * inv_rows * gain_of[c]).astype(bf16)

    def own_lines(ref):
        return ref[pl.ds(0, LINES, stride=NZ), :]

    def hidden_forward(e, pre_e, g):
        pre = x_total(pre_e) * inv_rms(e)
        x_gather(g, (pre / (1.0 + jnp.exp(-pre))).astype(bf16))

    def branch_forward(r, g):
        branch = t_dot(x_gathered(g), wd[...].reshape(NX * UNITS, SLICE))
        for c in range(BLOCKS):
            fs[r, pl.ds(c * 128, 128), :] = branch[:, block(c)]
        sum_first(r)

    def pre_backward(e, pre_e, tick):
        inv = inv_rms(e)
        pre = x_total(pre_e) * inv
        sig = 1.0 / (1.0 + jnp.exp(-pre))
        hid[:, tick * ROWS : (tick + 1) * ROWS] = (pre * sig).astype(bf16)
        return inv, pre, sig * (1.0 + pre * (1.0 - sig))

    def d_pre_backward(tick, dh_e, g, pre, slope):
        d_pre = (x_total(dh_e) * slope).astype(bf16)
        x_gather(g, d_pre)
        dpre[:, tick * ROWS : (tick + 1) * ROWS] = d_pre
        mm[tick, 0] = jnp.broadcast_to(jnp.sum(d_pre.astype(f32) * pre, axis=0, keepdims=True), (8, 128))
        for d in (2, 1, 3):
            send(mm.at[tick, 0], mm.at[tick, NX - d], mms.at[tick], mmr.at[tick], at_x(d))

    def branch_backward(r, g, e, tick, inv, inv_rows):
        d_norm = t_dot(x_gathered(g), wu[...].reshape(NX * UNITS, SLICE))
        wait_bytes(mm.at[tick, pl.ds(1, NX - 1)], mmr.at[tick])
        total = (mm[tick, 0] + mm[tick, 1] + mm[tick, 2] + mm[tick, 3])[0:1, :]
        back = by_row(total * inv * inv * (1.0 / WIDTH))
        for c in range(BLOCKS):
            x = xs[e, pl.ds(c * 128, 128), :]
            part = d_norm[:, block(c)] * inv_rows
            fs[r, pl.ds(c * 128, 128), :] = part * gain_of[c] - x * back
            line = jnp.sum(part * x, axis=0, keepdims=True)
            if tick == 0:
                gpart[c : c + 1, :] = line
            else:
                gpart[c : c + 1, :] += line
        sum_first(r)

    def hand_on(k, value, section, a):
        pas[k] = value
        pl.semaphore_wait(ready.at[k], 1)
        z_first(pas.at[k], gat.at[a], zs.at[a], zr.at[a], section)
        send(pas.at[k], gat.at[a, 0], ps.at[k], pr.at[k], at_z(0, section))

    def results_out(q, value):
        resf[q] = value
        for x in range(NX):
            ro[q, x] = jnp.concatenate(
                [resf[q, pl.ds(8 * c + 2 * x, 2), :] for c in range(BLOCKS)] + [jnp.zeros((6, 128), f32)], axis=0
            ).astype(bf16)
        for d in (2, 1, 3):
            send(ro.at[q, lax.rem(mx + d, NX)], ri.at[q, NX - d], rs.at[q], rr.at[q], at_x(d))
        ri[q, 0] = ro[q, mx]

    def results_in(q, ref, tick):
        wait_bytes(ri.at[q, pl.ds(1, NX - 1)], rr.at[q])
        for x in range(NX):
            got = ri[q, rel(x)].astype(f32)
            for c in range(BLOCKS):
                col = (x * BLOCKS + c) * 128
                ref[tick, 0, :, col : col + 128] = got[2 * c : 2 * c + 2, :].astype(bf16)

    stores = []

    def weight_grad(left, n, grads, hbm):
        wait_bytes(full.at[n, pl.ds(1, NX - 1)], fur.at[n])
        wait_bytes(full.at[2 + n, pl.ds(1, NX - 1)], fur.at[2 + n])
        for x in range(NX):
            both = jnp.concatenate([full[n, x], full[2 + n, x]], axis=0)
            grads[x] = (dot(left[...], both) * 0.5).astype(bf16)
            where = slice_of(lax.rem(mx + x, NX))
            stores.append(pltpu.make_async_copy(grads.at[x], hbm.at[0, :, where], og_sem.at[n, x]))
            stores[-1].start()

    first_lines = lines[4].astype(bf16)
    loss_lines = lines[5].astype(bf16)
    gather_relay(ACT0)
    gather_relay(X0)
    gather_relay(DY0)
    gather_first(X1)
    take_input(ACT0, IN_F0, 0)
    own_up.wait()
    wait_bytes(wu.at[pl.ds(1, NX - 1)], wr.at[0])
    x_parts(PRE_F0, wu, xg[IN_F0])
    take_input(X0, IN_B0, 2)
    x_parts(PRE_B0, wu, xg[IN_B0])
    take_grad(DY0, 0, 2)
    own_down.wait()
    wait_bytes(wd.at[pl.ds(1, NX - 1)], wr.at[1])
    x_parts(DH_B0, wd, dyb[0])
    hidden_forward(IN_F0, PRE_F0, 1)
    inv, pre, slope = pre_backward(IN_B0, PRE_B0, 0)
    d_pre_backward(0, DH_B0, 0, pre, slope)
    gather_relay(X1)
    inv_rows = by_row(inv)
    spread_full(0, normed_block(IN_B0, inv_rows))
    branch_forward(F0, 1)
    branch_backward(B0, 0, IN_B0, 0, inv, inv_rows)
    take_input(X1, IN_B1, 3)
    x_parts(PRE_B1, wu, xg[IN_B1])
    sum_relay(F0)
    sum_relay(B0)
    spread_full(1, lambda c: dyb[0, :, block(c)])
    out = (sum_done(F0) + own_lines(xs.at[IN_F0])).astype(bf16)
    hand_on(0, jnp.where(sec == 7, first_lines, out), after, ACT1)
    grad = (sum_done(B0) + lines[0]).astype(bf16)
    hand_on(1, jnp.where(sec == 0, loss_lines, grad), before, DY1)

    results_out(0, out.astype(f32))
    results_out(1, grad.astype(f32))
    inv, pre, slope = pre_backward(IN_B1, PRE_B1, 1)
    inv_rows = by_row(inv)
    spread_full(2, normed_block(IN_B1, inv_rows))
    gather_relay(ACT1)
    gather_relay(DY1)
    wait_bytes(gat.at[ACT1, 0], pr.at[0])
    take_input(ACT1, IN_F1, 1)
    x_parts(PRE_F1, wu, xg[IN_F1])
    wait_bytes(gat.at[DY1, 0], pr.at[1])
    take_grad(DY1, 1, 3)
    x_parts(DH_B1, wd, dyb[1])
    hidden_forward(IN_F1, PRE_F1, 3)
    d_pre_backward(1, DH_B1, 2, pre, slope)
    spread_full(3, lambda c: dyb[1, :, block(c)])
    branch_forward(F1, 3)
    branch_backward(B1, 2, IN_B1, 1, inv, inv_rows)
    gz[0] = jnp.concatenate([gpart[...], jnp.zeros((8 - BLOCKS, 128), f32)], axis=0)
    z_first(gz.at[0], gz, gs.at[0], gr)
    sum_relay(F1)
    sum_relay(B1)
    z_relay(gz, gs.at[0], gr)
    weight_grad(dpre, 0, upg, upg_hbm)
    results_in(0, out_ref, 0)
    results_in(1, grad_ref, 0)
    results_out(3, sum_done(F1) + own_lines(xs.at[IN_F1]))
    results_out(2, sum_done(B1) + lines[1])
    z_near(gz, gr)
    z_far(gz, gr)
    total = jnp.zeros((8, 128), f32)
    for z in range(NZ):
        total = total + gz[lax.rem(z - mz + NZ, NZ)]
    gx[0] = total
    for d in (2, 1, 3):
        send(gx.at[0], gx.at[NX - d], gs.at[1], gr.at[7], at_x(d))

    weight_grad(hid, 1, downg, downg_hbm)
    results_in(2, grad_ref, 1)
    results_in(3, out_ref, 1)
    wait_bytes(gx.at[pl.ds(1, NX - 1)], gr.at[7])
    for x in range(NX):
        got = gx[rel(x)]
        for c in range(BLOCKS):
            col = (x * BLOCKS + c) * 128
            gaing_ref[:, col : col + 128] = got[c : c + 1, :]

    three = pl.ds(1, NX - 1)
    wait_bytes(msg_in.at[three], ms.at[0])
    wait_bytes(wu.at[three], ws.at[0])
    wait_bytes(wd.at[three], ws.at[1])
    for a in range(6):
        wait_bytes(gat.at[a, pl.ds(1, NZ - 1)], zs.at[a])
        wait_bytes(xi.at[a, three], xsn.at[a])
    for r in range(4):
        wait_bytes(wire.at[r, pl.ds(1, NZ - 1)], zs2.at[r])
        wait_bytes(sq.at[r, three], sqs.at[r])
        wait_bytes(ag.at[r, three], ags.at[r])
        wait_bytes(full.at[r, three], fus.at[r])
        wait_bytes(ri.at[r, three], rs.at[r])
    for k in range(2):
        wait_bytes(mm.at[k, three], mms.at[k])
        wait_bytes(pas.at[k], ps.at[k])
    wait_bytes(gz.at[pl.ds(1, NZ - 1)], gs.at[0])
    wait_bytes(gx.at[three], gs.at[1])
    for store in stores:
        store.wait()


def place(*refs):
    sources, targets, held, sem = refs[:5], refs[5:10], refs[10:15], refs[15]
    loads, stores = [], []
    for k in range(5):
        loads.append(pltpu.make_async_copy(sources[k], held[k], sem.at[0, k]))
        loads[k].start()
    for k in range(5):
        loads[k].wait()
        stores.append(pltpu.make_async_copy(held[k], targets[k], sem.at[1, k]))
        stores[k].start()
    for store in stores:
        store.wait()


def on_device(*args):
    vmem = pl.BlockSpec(memory_space=pltpu.VMEM)
    anywhere = pl.BlockSpec(memory_space=pl.ANY)
    dma = pltpu.SemaphoreType.DMA
    shapes = (
        jax.ShapeDtypeStruct((2, 1, 2, WIDTH), bf16),
        jax.ShapeDtypeStruct((2, 1, 2, WIDTH), bf16),
        jax.ShapeDtypeStruct((1, UNITS, WIDTH), bf16),
        jax.ShapeDtypeStruct((1, UNITS, WIDTH), bf16),
        jax.ShapeDtypeStruct((1, WIDTH), f32),
    )
    results = pl.pallas_call(
        kernel,
        out_shape=shapes,
        in_specs=[vmem] * 8 + [anywhere] * 2,
        out_specs=(vmem, vmem, anywhere, anywhere, vmem),
        scratch_shapes=[
            pltpu.VMEM((NX, UNITS, SLICE), bf16),
            pltpu.VMEM((NX, UNITS, SLICE), bf16),
            pltpu.VMEM((NX, 64, 128), f32),
            pltpu.VMEM((NX, 64, 128), bf16),
            pltpu.VMEM((NX, 64, 128), bf16),
            pltpu.VMEM((6, LINES, 128), f32),
            pltpu.VMEM((6, NZ, LINES, 128), bf16),
            pltpu.VMEM((SLICE, 128), f32),
            pltpu.VMEM((4, SLICE, 128), f32),
            pltpu.VMEM((4, ROWS, SLICE), bf16),
            pltpu.VMEM((2, ROWS, SLICE), bf16),
            pltpu.VMEM((4, SLICE, 128), f32),
            pltpu.VMEM((4, NZ, LINES, 128), bf16),
            pltpu.VMEM((4, 7, LINES, 128), bf16),
            pltpu.VMEM((4, 8, LINES, 128), bf16),
            pltpu.VMEM((6, UNITS, ROWS), f32),
            pltpu.VMEM((6, NX, UNITS, ROWS), bf16),
            pltpu.VMEM((6, NX, UNITS, ROWS), bf16),
            pltpu.VMEM((4, NX, 8, 128), f32),
            pltpu.VMEM((4, NX, UNITS, ROWS), bf16),
            pltpu.VMEM((2, NX, 8, 128), f32),
            pltpu.VMEM((4, NX, ROWS, SLICE), bf16),
            pltpu.VMEM((UNITS, 2 * ROWS), bf16),
            pltpu.VMEM((UNITS, 2 * ROWS), bf16),
            pltpu.VMEM((BLOCKS, 128), f32),
            pltpu.VMEM((NZ, 8, 128), f32),
            pltpu.VMEM((NX, 8, 128), f32),
            pltpu.VMEM((2, LINES, 128), bf16),
            pltpu.VMEM((4, LINES, 128), f32),
            pltpu.VMEM((4, NX, 16, 128), bf16),
            pltpu.VMEM((4, NX, 16, 128), bf16),
            pltpu.VMEM((4, ROWS, ROWS), bf16),
            pltpu.VMEM((NX, UNITS, SLICE), bf16),
            pltpu.VMEM((NX, UNITS, SLICE), bf16),
            dma((2,)),
            dma((2,)),
            dma((2,)),
            dma((1,)),
            dma((1,)),
            dma((6,)),
            dma((6, 7)),
            dma((4,)),
            dma((4, 2)),
            dma((6,)),
            dma((6,)),
            dma((4,)),
            dma((4,)),
            dma((4,)),
            dma((4,)),
            dma((2,)),
            dma((2,)),
            dma((4,)),
            dma((4,)),
            dma((2,)),
            dma((2,)),
            dma((4,)),
            dma((4,)),
            dma((2,)),
            dma((8,)),
            dma((2, NX)),
            pltpu.SemaphoreType.REGULAR((2,)),
        ],
        compiler_params=pltpu.CompilerParams(
            collective_id=0, has_side_effects=True, vmem_limit_bytes=56 * 1024 * 1024
        ),
    )(*args)
    return pl.pallas_call(
        place,
        out_shape=shapes,
        in_specs=[anywhere] * 5,
        out_specs=(anywhere,) * 5,
        scratch_shapes=[pltpu.VMEM(shape.shape, shape.dtype) for shape in shapes] + [dma((2, 5))],
    )(*results)


def solution(mesh):
    placed = (
        P("section", "peer", None),
        P(None, "peer", None),
        P(None, "section", "peer", None),
        P("section", "peer", None),
        P(None, "peer", None),
        P(),
        P(),
        P("section", None),
        P("section", "peer", None),
        P("section", "peer", None),
    )
    return jax.shard_map(
        on_device,
        mesh=mesh,
        in_specs=placed,
        out_specs=(
            P(None, "section", "peer", None),
            P(None, "section", "peer", None),
            P("section", "peer", None),
            P("section", "peer", None),
            P("section", None),
        ),
        check_vma=False,
    )
```

```python
import jax
import jax.numpy as jnp
from jax import lax
from jax.experimental import pallas as pl
from jax.experimental.pallas import tpu as pltpu
from jax.sharding import PartitionSpec as P

MESH = pl.DeviceIdType.MESH
EPS = 1e-05
NX, NZ = 4, 16
ROWS = 128
BLOCKS = 5
SLICE = BLOCKS * 128
WIDTH = NX * SLICE
LINES = 8 * BLOCKS
PAIR = 2 * BLOCKS
UNITS = 160
X0, DY0, ACT0, X1, ACT1, DY1 = range(6)
B0, F0, B1, F1 = range(4)
PRE_B0, DH_B0, PRE_F0, PRE_B1, DH_B1, PRE_F1 = range(6)
IN_B0, IN_F0, IN_B1, IN_F1 = range(4)
f32, bf16 = jnp.float32, jnp.bfloat16


def dot(a, b):
    return jnp.dot(a, b, preferred_element_type=f32)


def dot_t(a, b):
    return lax.dot_general(a, b, (((1,), (1,)), ((), ())), preferred_element_type=f32)


def t_dot(a, b):
    return lax.dot_general(a, b, (((0,), (0,)), ((), ())), preferred_element_type=f32)


def wait_bytes(ref, sem):
    pltpu.make_async_copy(ref, ref, sem).wait()


def kernel(
    act_hbm, first_hbm, stored_hbm, pend_hbm, loss_hbm, fw_hbm, bw_hbm, gain_hbm, up_hbm, down_hbm,
    out_ref, grad_ref, upg_hbm, downg_hbm, gaing_ref,
    act_ref, first_ref, stored_ref, pend_ref, loss_ref, fw_ref, bw_ref, gain_ref, wu, wd, msgf, msg_out, msg_in, lines, gat, nat, xs, xg, dyb, fs, wire, rin, fin,
    xown, xo, xi, sq, ag, mm, full, hid, dpre, gpart, gz, gx, pas, resf, ro, ri, hot, upg, downg,
    w_sem, ws, wr, ms, mr, zs, zr, zs2, zr2, xsn, xrc, sqs, sqr, ags, agr, mms, mmr, fus, fur, ps, pr, rs, rr,
    gs, gr, og_sem, ready,
):
    sec = lax.axis_index("section")
    peer = lax.axis_index("peer")
    mx, mz = peer // NZ, lax.rem(peer, NZ)
    even = lax.rem(mz, 2) == 0

    after, before = lax.rem(sec + 1, 8), lax.rem(sec + 7, 8)

    def at_z(d, section=sec):
        return (section, mx * NZ + lax.rem(mz + (d + NZ), NZ))

    def at_x(d):
        return (sec, lax.rem(mx + d, NX) * NZ + mz)

    def send(src, dst, ssem, rsem, dev):
        pltpu.make_async_remote_copy(
            src_ref=src, dst_ref=dst, send_sem=ssem, recv_sem=rsem, device_id=dev, device_id_type=MESH
        ).start()

    def slice_of(x):
        return pl.ds(pl.multiple_of(x * SLICE, 128), SLICE)

    def rel(x):
        return lax.rem(x - mx + NX, NX)

    barrier = pltpu.get_barrier_semaphore()
    steps = (1, 2, 3, 4, -1, -2, -3, -4)
    greeted = [at_z(d) for d in steps] + [at_x(d) for d in (1, 2, 3)] + [at_z(0, after), at_z(0, before)]
    for other in greeted:
        pl.semaphore_signal(barrier, inc=1, device_id=other, device_id_type=MESH)

    loads = [
        pltpu.make_async_copy(source, target, w_sem.at[2 + n])
        for n, (source, target) in enumerate(
            (
                (stored_hbm, stored_ref), (pend_hbm, pend_ref), (act_hbm, act_ref), (first_hbm, first_ref),
                (loss_hbm, loss_ref), (fw_hbm, fw_ref), (bw_hbm, bw_ref), (gain_hbm, gain_ref),
            )
        )
    ]
    for load in loads:
        load.start()

    own_up = pltpu.make_async_copy(up_hbm.at[0, :, slice_of(mx)], wu.at[0], w_sem.at[0])
    own_down = pltpu.make_async_copy(down_hbm.at[0, :, slice_of(mx)], wd.at[0], w_sem.at[1])
    own_up.start()
    own_down.start()

    for load in loads:
        load.wait()

    pairs = [stored_ref[0, 0], pend_ref[0], act_ref[0], stored_ref[1, 0], first_ref[0], loss_ref[0]]
    for x in range(NX):
        msgf[x, pl.ds(56, 8), :] = jnp.zeros((8, 128), f32)
    for a, pair in enumerate(pairs):
        flat = pair.astype(f32)
        for x in range(NX):
            for c in range(BLOCKS):
                col = (x * BLOCKS + c) * 128
                msgf[x, pl.ds(a * PAIR + 2 * c, 2), :] = flat[:, col : col + 128]
    for x in range(NX):
        msg_out[x] = msgf[x].astype(bf16)
    pl.semaphore_wait(barrier, len(greeted))
    pl.semaphore_signal(ready.at[0], inc=1, device_id=at_z(0, before), device_id_type=MESH)
    pl.semaphore_signal(ready.at[1], inc=1, device_id=at_z(0, after), device_id_type=MESH)

    for d in (2, 1, 3):
        send(msg_out.at[lax.rem(mx + d, NX)], msg_in.at[NX - d], ms.at[0], mr.at[0], at_x(d))
    for k, (src, dst) in enumerate(((up_hbm, wu), (down_hbm, wd))):
        for d in (2, 1, 3):
            send(src.at[0, :, slice_of(lax.rem(mx + d, NX))], dst.at[NX - d], ws.at[k], wr.at[k], at_x(d))
    msg_in[0] = msg_out[mx]
    wait_bytes(msg_in.at[pl.ds(1, NX - 1)], mr.at[0])

    def take_lines(arrays):
        for x in range(NX):
            got = msg_in[rel(x)].astype(f32)
            for a in arrays:
                for c in range(BLOCKS):
                    lines[a, pl.ds(8 * c + 2 * x, 2), :] = got[a * PAIR + 2 * c : a * PAIR + 2 * c + 2, :]

    def z_first(src, buf, ssem, rsem, section=sec):
        send(src, buf.at[12], ssem, rsem.at[0], at_z(4, section))
        send(src, buf.at[4], ssem, rsem.at[1], at_z(-4, section))
        for d in (3, 2, 1):
            send(src, buf.at[NZ - d], ssem, rsem.at[2], at_z(d, section))
            send(src, buf.at[d], ssem, rsem.at[3], at_z(-d, section))

    def z_relay(buf, ssem, rsem):
        wait_bytes(buf.at[12], rsem.at[0])
        wait_bytes(buf.at[4], rsem.at[1])
        send(buf.at[jnp.where(even, 12, 4)], buf.at[8], ssem, rsem.at[4], at_z(jnp.where(even, 4, -4)))
        for d in (3, 2, 1):
            send(buf.at[12], buf.at[12 - d], ssem, rsem.at[5], at_z(d))
            send(buf.at[4], buf.at[4 + d], ssem, rsem.at[6], at_z(-d))

    def z_near(buf, rsem):
        wait_bytes(buf.at[pl.ds(13, 3)], rsem.at[2])
        wait_bytes(buf.at[pl.ds(1, 3)], rsem.at[3])

    def z_far(buf, rsem):
        wait_bytes(buf.at[8], rsem.at[4])
        wait_bytes(buf.at[pl.ds(9, 3)], rsem.at[5])
        wait_bytes(buf.at[pl.ds(5, 3)], rsem.at[6])

    def gather_first(a):
        z_first(gat.at[a, 0], gat.at[a], zs.at[a], zr.at[a])

    def gather_relay(a):
        z_relay(gat.at[a], zs.at[a], zr.at[a])

    take_lines((X0, DY0))
    for a in (X0, DY0):
        gat[a, 0] = lines[a].astype(bf16)
        gather_first(a)
    take_lines((ACT0, X1, 4, 5))
    gat[ACT0, 0] = lines[ACT0].astype(bf16)
    gather_first(ACT0)
    gat[X1, 0] = lines[X1].astype(bf16)

    def sum_first(r):
        def fill(k):
            wire[r, k] = fs[r, pl.ds(k, LINES, stride=NZ), :].astype(bf16)

        fill(8)
        send(wire.at[r, 8], rin.at[r, 6], zs2.at[r], zr2.at[r, 0], at_z(jnp.where(even, 4, -4)))
        for d in (3, 2, 1):
            fill(4 + d)
            send(wire.at[r, 4 + d], rin.at[r, d - 1], zs2.at[r], zr2.at[r, 0], at_z(d))
            fill(12 - d)
            send(wire.at[r, 12 - d], rin.at[r, 2 + d], zs2.at[r], zr2.at[r, 0], at_z(-d))
        for d in (3, 2, 1):
            fill(d)
            send(wire.at[r, d], fin.at[r, d - 1], zs2.at[r], zr2.at[r, 1], at_z(d))
            fill(NZ - d)
            send(wire.at[r, NZ - d], fin.at[r, 2 + d], zs2.at[r], zr2.at[r, 1], at_z(-d))

    def sum_relay(r):
        ahead = fs[r, pl.ds(4, LINES, stride=NZ), :]
        behind = fs[r, pl.ds(12, LINES, stride=NZ), :]
        wait_bytes(rin.at[r], zr2.at[r, 0])
        across = rin[r, 6].astype(f32)
        for k in range(3):
            ahead = ahead + rin[r, k].astype(f32)
            behind = behind + rin[r, 3 + k].astype(f32)
        wire[r, 4] = (ahead + jnp.where(even, across, 0.0)).astype(bf16)
        wire[r, 12] = (behind + jnp.where(even, 0.0, across)).astype(bf16)
        send(wire.at[r, 4], fin.at[r, 6], zs2.at[r], zr2.at[r, 1], at_z(4))
        send(wire.at[r, 12], fin.at[r, 7], zs2.at[r], zr2.at[r, 1], at_z(-4))

    def sum_done(r):
        total = fs[r, pl.ds(0, LINES, stride=NZ), :]
        wait_bytes(fin.at[r], zr2.at[r, 1])
        for k in range(8):
            total = total + fin[r, k].astype(f32)
        return total

    def row_of(index):
        group = index // NZ
        return 2 * ((group // 2) * NZ + lax.rem(mz + lax.rem(index, NZ), NZ)) + lax.rem(group, 2)

    lane = lax.broadcasted_iota(jnp.int32, (ROWS, ROWS), 1)
    placed = row_of(lax.broadcasted_iota(jnp.int32, (ROWS, ROWS), 0)) == lane
    lane_row = row_of(lane).astype(f32)

    def one_hot(route):
        picked = jnp.sum(jnp.where(placed, route.astype(f32), 0.0), axis=1, keepdims=True)
        return jnp.where(picked == lane_row, 1.0, 0.0)

    for tick in range(2):
        hot[tick] = one_hot(fw_ref[tick, pl.ds(sec, 1), :]).astype(bf16)
        hot[2 + tick] = one_hot(bw_ref[tick, pl.ds(sec, 1), :]).T.astype(bf16)

    gain = gain_ref[:, slice_of(mx)]
    gain_of = [gain[:, c * 128 : (c + 1) * 128] for c in range(BLOCKS)]

    def block(c):
        return slice(c * 128, (c + 1) * 128)

    def turned(a, index):
        z_near(gat.at[a], zr.at[a])
        for k in (0, 1, 2, 3, 4, 12, 13, 14, 15):
            nat[pl.ds(k, LINES, stride=NZ), :] = gat[a, k].astype(f32)
        z_far(gat.at[a], zr.at[a])
        for k in range(5, 12):
            nat[pl.ds(k, LINES, stride=NZ), :] = gat[a, k].astype(f32)
        both = jnp.concatenate([nat[pl.ds(c * 128, 128), :] for c in range(BLOCKS)], axis=1)
        return dot(hot[index], both.astype(bf16))

    def take_input(a, e, index):
        got = turned(a, index)
        total = jnp.zeros((ROWS, 128), f32)
        for c in range(BLOCKS):
            part = got[:, block(c)]
            xs[e, pl.ds(c * 128, 128), :] = part
            xg[e, :, block(c)] = (part * gain_of[c]).astype(bf16)
            total = total + part * part
        sq[e, 0] = jnp.broadcast_to(jnp.sum(total.T, axis=0, keepdims=True), (8, 128))
        for d in (2, 1, 3):
            send(sq.at[e, 0], sq.at[e, NX - d], sqs.at[e], sqr.at[e], at_x(d))

    def take_grad(a, tick, index):
        got = turned(a, index)
        dyb[tick] = got.astype(bf16)
        for c in range(BLOCKS):
            lines[tick, pl.ds(8 * c, 8), :] = jnp.concatenate(
                [got[16 * k : 16 * k + 1, block(c)] for k in range(8)], axis=0
            )

    def x_parts(e, weight, rows):
        parts = dot_t(weight[...].reshape(NX * UNITS, SLICE), rows)
        for d in (2, 1, 3):
            xo[e, d] = parts[d * UNITS : (d + 1) * UNITS, :].astype(bf16)
            send(xo.at[e, d], xi.at[e, NX - d], xsn.at[e], xrc.at[e], at_x(d))
        xown[e] = parts[:UNITS, :]

    def x_total(e):
        wait_bytes(xi.at[e, pl.ds(1, NX - 1)], xrc.at[e])
        total = xown[e]
        for k in range(1, NX):
            total = total + xi[e, k].astype(f32)
        return total

    def x_gather(g, value):
        ag[g, 0] = value
        for d in (2, 1, 3):
            send(ag.at[g, 0], ag.at[g, NX - d], ags.at[g], agr.at[g], at_x(d))

    def x_gathered(g):
        wait_bytes(ag.at[g, pl.ds(1, NX - 1)], agr.at[g])
        return ag[g].reshape(NX * UNITS, ROWS)

    def inv_rms(e):
        wait_bytes(sq.at[e, pl.ds(1, NX - 1)], sqr.at[e])
        total = sq[e, 0] + sq[e, 1] + sq[e, 2] + sq[e, 3]
        return lax.rsqrt(total[0:1, :] * (1.0 / WIDTH) + EPS)

    def by_row(value):
        return jnp.broadcast_to(value, (ROWS, ROWS)).T

    def spread_full(n, value):
        for c in range(BLOCKS):
            full[n, 0, :, block(c)] = value(c)
        for d in (2, 1, 3):
            send(full.at[n, 0], full.at[n, NX - d], fus.at[n], fur.at[n], at_x(d))

    def normed_block(e, inv_rows):
        return lambda c: (xs[e, pl.ds(c * 128, 128), :] * inv_rows * gain_of[c]).astype(bf16)

    def own_lines(ref):
        return ref[pl.ds(0, LINES, stride=NZ), :]

    def hidden_forward(e, pre_e, g):
        pre = x_total(pre_e) * inv_rms(e)
        x_gather(g, (pre / (1.0 + jnp.exp(-pre))).astype(bf16))

    def branch_forward(r, g):
        branch = t_dot(x_gathered(g), wd[...].reshape(NX * UNITS, SLICE))
        for c in range(BLOCKS):
            fs[r, pl.ds(c * 128, 128), :] = branch[:, block(c)]
        sum_first(r)

    def pre_backward(e, pre_e, tick):
        inv = inv_rms(e)
        pre = x_total(pre_e) * inv
        sig = 1.0 / (1.0 + jnp.exp(-pre))
        hid[:, tick * ROWS : (tick + 1) * ROWS] = (pre * sig).astype(bf16)
        return inv, pre, sig * (1.0 + pre * (1.0 - sig))

    def d_pre_backward(tick, dh_e, g, pre, slope):
        d_pre = (x_total(dh_e) * slope).astype(bf16)
        x_gather(g, d_pre)
        dpre[:, tick * ROWS : (tick + 1) * ROWS] = d_pre
        mm[tick, 0] = jnp.broadcast_to(jnp.sum(d_pre.astype(f32) * pre, axis=0, keepdims=True), (8, 128))
        for d in (2, 1, 3):
            send(mm.at[tick, 0], mm.at[tick, NX - d], mms.at[tick], mmr.at[tick], at_x(d))

    def branch_backward(r, g, e, tick, inv, inv_rows):
        d_norm = t_dot(x_gathered(g), wu[...].reshape(NX * UNITS, SLICE))
        wait_bytes(mm.at[tick, pl.ds(1, NX - 1)], mmr.at[tick])
        total = (mm[tick, 0] + mm[tick, 1] + mm[tick, 2] + mm[tick, 3])[0:1, :]
        back = by_row(total * inv * inv * (1.0 / WIDTH))
        for c in range(BLOCKS):
            x = xs[e, pl.ds(c * 128, 128), :]
            part = d_norm[:, block(c)] * inv_rows
            fs[r, pl.ds(c * 128, 128), :] = part * gain_of[c] - x * back
            line = jnp.sum(part * x, axis=0, keepdims=True)
            if tick == 0:
                gpart[c : c + 1, :] = line
            else:
                gpart[c : c + 1, :] += line
        if tick == 1:
            gz[0] = jnp.concatenate([gpart[...], jnp.zeros((8 - BLOCKS, 128), f32)], axis=0)
            z_first(gz.at[0], gz, gs.at[0], gr)
        sum_first(r)

    def hand_on(k, value, section, a):
        pas[k] = value
        pl.semaphore_wait(ready.at[k], 1)
        z_first(pas.at[k], gat.at[a], zs.at[a], zr.at[a], section)
        send(pas.at[k], gat.at[a, 0], ps.at[k], pr.at[k], at_z(0, section))

    def results_out(q, value):
        resf[q] = value
        for x in range(NX):
            ro[q, x] = jnp.concatenate(
                [resf[q, pl.ds(8 * c + 2 * x, 2), :] for c in range(BLOCKS)] + [jnp.zeros((6, 128), f32)], axis=0
            ).astype(bf16)
        for d in (2, 1, 3):
            send(ro.at[q, lax.rem(mx + d, NX)], ri.at[q, NX - d], rs.at[q], rr.at[q], at_x(d))
        ri[q, 0] = ro[q, mx]

    def results_in(q, ref, tick):
        wait_bytes(ri.at[q, pl.ds(1, NX - 1)], rr.at[q])
        for x in range(NX):
            got = ri[q, rel(x)].astype(f32)
            for c in range(BLOCKS):
                col = (x * BLOCKS + c) * 128
                ref[tick, 0, :, col : col + 128] = got[2 * c : 2 * c + 2, :].astype(bf16)

    stores = []

    def weight_grad(left, n, grads, hbm):
        wait_bytes(full.at[n, pl.ds(1, NX - 1)], fur.at[n])
        wait_bytes(full.at[2 + n, pl.ds(1, NX - 1)], fur.at[2 + n])
        for x in range(NX):
            both = jnp.concatenate([full[n, x], full[2 + n, x]], axis=0)
            grads[x] = (dot(left[...], both) * 0.5).astype(bf16)
            where = slice_of(lax.rem(mx + x, NX))
            stores.append(pltpu.make_async_copy(grads.at[x], hbm.at[0, :, where], og_sem.at[n, x]))
            stores[-1].start()

    first_lines = lines[4].astype(bf16)
    loss_lines = lines[5].astype(bf16)
    gather_relay(X0)
    gather_relay(DY0)
    gather_relay(ACT0)
    take_input(X0, IN_B0, 2)
    own_up.wait()
    wait_bytes(wu.at[pl.ds(1, NX - 1)], wr.at[0])
    x_parts(PRE_B0, wu, xg[IN_B0])
    take_grad(DY0, 0, 2)
    own_down.wait()
    wait_bytes(wd.at[pl.ds(1, NX - 1)], wr.at[1])
    x_parts(DH_B0, wd, dyb[0])
    take_input(ACT0, IN_F0, 0)
    x_parts(PRE_F0, wu, xg[IN_F0])
    gather_first(X1)
    inv, pre, slope = pre_backward(IN_B0, PRE_B0, 0)
    d_pre_backward(0, DH_B0, 0, pre, slope)
    hidden_forward(IN_F0, PRE_F0, 1)
    inv_rows = by_row(inv)
    spread_full(0, normed_block(IN_B0, inv_rows))
    gather_relay(X1)
    branch_backward(B0, 0, IN_B0, 0, inv, inv_rows)
    branch_forward(F0, 1)
    take_input(X1, IN_B1, 3)
    x_parts(PRE_B1, wu, xg[IN_B1])
    sum_relay(B0)
    sum_relay(F0)
    spread_full(1, lambda c: dyb[0, :, block(c)])
    grad = (sum_done(B0) + lines[0]).astype(bf16)
    hand_on(1, jnp.where(sec == 0, loss_lines, grad), before, DY1)
    out = (sum_done(F0) + own_lines(xs.at[IN_F0])).astype(bf16)
    hand_on(0, jnp.where(sec == 7, first_lines, out), after, ACT1)

    inv, pre, slope = pre_backward(IN_B1, PRE_B1, 1)
    inv_rows = by_row(inv)
    results_out(1, grad.astype(f32))
    results_out(0, out.astype(f32))
    gather_relay(DY1)
    gather_relay(ACT1)
    spread_full(2, normed_block(IN_B1, inv_rows))
    wait_bytes(gat.at[DY1, 0], pr.at[1])
    take_grad(DY1, 1, 3)
    x_parts(DH_B1, wd, dyb[1])
    wait_bytes(gat.at[ACT1, 0], pr.at[0])
    take_input(ACT1, IN_F1, 1)
    x_parts(PRE_F1, wu, xg[IN_F1])
    d_pre_backward(1, DH_B1, 2, pre, slope)
    hidden_forward(IN_F1, PRE_F1, 3)
    spread_full(3, lambda c: dyb[1, :, block(c)])
    branch_backward(B1, 2, IN_B1, 1, inv, inv_rows)
    branch_forward(F1, 3)
    z_relay(gz, gs.at[0], gr)
    sum_relay(B1)
    sum_relay(F1)
    weight_grad(dpre, 0, upg, upg_hbm)
    results_in(0, out_ref, 0)
    results_in(1, grad_ref, 0)
    results_out(2, sum_done(B1) + lines[1])
    z_near(gz, gr)
    z_far(gz, gr)
    total = jnp.zeros((8, 128), f32)
    for z in range(NZ):
        total = total + gz[lax.rem(z - mz + NZ, NZ)]
    gx[0] = total
    for d in (2, 1, 3):
        send(gx.at[0], gx.at[NX - d], gs.at[1], gr.at[7], at_x(d))
    results_out(3, sum_done(F1) + own_lines(xs.at[IN_F1]))

    weight_grad(hid, 1, downg, downg_hbm)
    results_in(2, grad_ref, 1)
    results_in(3, out_ref, 1)
    wait_bytes(gx.at[pl.ds(1, NX - 1)], gr.at[7])
    for x in range(NX):
        got = gx[rel(x)]
        for c in range(BLOCKS):
            col = (x * BLOCKS + c) * 128
            gaing_ref[:, col : col + 128] = got[c : c + 1, :]

    three = pl.ds(1, NX - 1)
    wait_bytes(msg_in.at[three], ms.at[0])
    wait_bytes(wu.at[three], ws.at[0])
    wait_bytes(wd.at[three], ws.at[1])
    for a in range(6):
        wait_bytes(gat.at[a, pl.ds(1, NZ - 1)], zs.at[a])
        wait_bytes(xi.at[a, three], xsn.at[a])
    for r in range(4):
        wait_bytes(wire.at[r, pl.ds(1, NZ - 1)], zs2.at[r])
        wait_bytes(sq.at[r, three], sqs.at[r])
        wait_bytes(ag.at[r, three], ags.at[r])
        wait_bytes(full.at[r, three], fus.at[r])
        wait_bytes(ri.at[r, three], rs.at[r])
    for k in range(2):
        wait_bytes(mm.at[k, three], mms.at[k])
        wait_bytes(pas.at[k], ps.at[k])
    wait_bytes(gz.at[pl.ds(1, NZ - 1)], gs.at[0])
    wait_bytes(gx.at[three], gs.at[1])
    for store in stores:
        store.wait()


def place(*refs):
    sources, targets, held, sem = refs[:5], refs[5:10], refs[10:15], refs[15]
    chunks = [(k, pl.ds(32 * n, 32)) for n in range(UNITS // 32) for k in (2, 3)]
    moves = [(sources[k].at[0, part], held[k].at[0, part], targets[k].at[0, part]) for k, part in chunks]
    moves += [(sources[k], held[k], targets[k]) for k in (0, 1, 4)]
    loads = [pltpu.make_async_copy(move[0], move[1], sem.at[0, n]) for n, move in enumerate(moves)]
    stores = [pltpu.make_async_copy(move[1], move[2], sem.at[1, n]) for n, move in enumerate(moves)]
    for load in loads:
        load.start()
    for load, store in zip(loads, stores):
        load.wait()
        store.start()
    for store in stores:
        store.wait()


def on_device(*args):
    vmem = pl.BlockSpec(memory_space=pltpu.VMEM)
    anywhere = pl.BlockSpec(memory_space=pl.ANY)
    dma = pltpu.SemaphoreType.DMA
    shapes = (
        jax.ShapeDtypeStruct((2, 1, 2, WIDTH), bf16),
        jax.ShapeDtypeStruct((2, 1, 2, WIDTH), bf16),
        jax.ShapeDtypeStruct((1, UNITS, WIDTH), bf16),
        jax.ShapeDtypeStruct((1, UNITS, WIDTH), bf16),
        jax.ShapeDtypeStruct((1, WIDTH), f32),
    )
    results = pl.pallas_call(
        kernel,
        out_shape=shapes,
        in_specs=[anywhere] * 10,
        out_specs=(vmem, vmem, anywhere, anywhere, vmem),
        scratch_shapes=[
            pltpu.VMEM((1, 2, WIDTH), bf16),
            pltpu.VMEM((1, 2, WIDTH), bf16),
            pltpu.VMEM((2, 1, 2, WIDTH), bf16),
            pltpu.VMEM((1, 2, WIDTH), bf16),
            pltpu.VMEM((1, 2, WIDTH), bf16),
            pltpu.VMEM((2, 8, ROWS), jnp.int32),
            pltpu.VMEM((2, 8, ROWS), jnp.int32),
            pltpu.VMEM((1, WIDTH), f32),
            pltpu.VMEM((NX, UNITS, SLICE), bf16),
            pltpu.VMEM((NX, UNITS, SLICE), bf16),
            pltpu.VMEM((NX, 64, 128), f32),
            pltpu.VMEM((NX, 64, 128), bf16),
            pltpu.VMEM((NX, 64, 128), bf16),
            pltpu.VMEM((6, LINES, 128), f32),
            pltpu.VMEM((6, NZ, LINES, 128), bf16),
            pltpu.VMEM((SLICE, 128), f32),
            pltpu.VMEM((4, SLICE, 128), f32),
            pltpu.VMEM((4, ROWS, SLICE), bf16),
            pltpu.VMEM((2, ROWS, SLICE), bf16),
            pltpu.VMEM((4, SLICE, 128), f32),
            pltpu.VMEM((4, NZ, LINES, 128), bf16),
            pltpu.VMEM((4, 7, LINES, 128), bf16),
            pltpu.VMEM((4, 8, LINES, 128), bf16),
            pltpu.VMEM((6, UNITS, ROWS), f32),
            pltpu.VMEM((6, NX, UNITS, ROWS), bf16),
            pltpu.VMEM((6, NX, UNITS, ROWS), bf16),
            pltpu.VMEM((4, NX, 8, 128), f32),
            pltpu.VMEM((4, NX, UNITS, ROWS), bf16),
            pltpu.VMEM((2, NX, 8, 128), f32),
            pltpu.VMEM((4, NX, ROWS, SLICE), bf16),
            pltpu.VMEM((UNITS, 2 * ROWS), bf16),
            pltpu.VMEM((UNITS, 2 * ROWS), bf16),
            pltpu.VMEM((BLOCKS, 128), f32),
            pltpu.VMEM((NZ, 8, 128), f32),
            pltpu.VMEM((NX, 8, 128), f32),
            pltpu.VMEM((2, LINES, 128), bf16),
            pltpu.VMEM((4, LINES, 128), f32),
            pltpu.VMEM((4, NX, 16, 128), bf16),
            pltpu.VMEM((4, NX, 16, 128), bf16),
            pltpu.VMEM((4, ROWS, ROWS), bf16),
            pltpu.VMEM((NX, UNITS, SLICE), bf16),
            pltpu.VMEM((NX, UNITS, SLICE), bf16),
            dma((10,)),
            dma((2,)),
            dma((2,)),
            dma((1,)),
            dma((1,)),
            dma((6,)),
            dma((6, 7)),
            dma((4,)),
            dma((4, 2)),
            dma((6,)),
            dma((6,)),
            dma((4,)),
            dma((4,)),
            dma((4,)),
            dma((4,)),
            dma((2,)),
            dma((2,)),
            dma((4,)),
            dma((4,)),
            dma((2,)),
            dma((2,)),
            dma((4,)),
            dma((4,)),
            dma((2,)),
            dma((8,)),
            dma((2, NX)),
            pltpu.SemaphoreType.REGULAR((2,)),
        ],
        compiler_params=pltpu.CompilerParams(
            collective_id=0, has_side_effects=True, vmem_limit_bytes=56 * 1024 * 1024
        ),
    )(*args)
    return pl.pallas_call(
        place,
        out_shape=shapes,
        in_specs=[anywhere] * 5,
        out_specs=(anywhere,) * 5,
        scratch_shapes=[pltpu.VMEM(shape.shape, shape.dtype) for shape in shapes] + [dma((2, 16))],
    )(*results)


def solution(mesh):
    placed = (
        P("section", "peer", None),
        P(None, "peer", None),
        P(None, "section", "peer", None),
        P("section", "peer", None),
        P(None, "peer", None),
        P(),
        P(),
        P("section", None),
        P("section", "peer", None),
        P("section", "peer", None),
    )
    return jax.shard_map(
        on_device,
        mesh=mesh,
        in_specs=placed,
        out_specs=(
            P(None, "section", "peer", None),
            P(None, "section", "peer", None),
            P("section", "peer", None),
            P("section", "peer", None),
            P("section", None),
        ),
        check_vma=False,
    )
```
